32 devices in a mesh: dom: 8 (over z, x), sub: 4 (over y, core).
Axes of the slice: x: 2, y: 2, z: 4, core: 2. Of those that a mesh axis runs over, the one named last changes fastest.
Arguments:
- directions: bfloat16 [384, 64, 128], P(('dom', 'sub')), may hold values from -6 to 6
- tiles: bfloat16 [384, 27, 128, 128], P(('dom', 'sub')), may hold values from -0.109375 to 0.109375
- tile_cols: int32 [384, 27], P(('dom', 'sub')), may hold values from 0 to 79
- friction: float32 [384, 128], P(('dom', 'sub')), may hold values from 0.3 to 3
- neighbours: int32 [8, 4], P('dom'), may hold values from -1 to 7, as said below
- send_idx: int32 [32, 4, 2], P(('dom', 'sub')), may hold values from 0 to 11
- send_count: int32 [32, 4], P(('dom', 'sub')), may hold values from 1 to 2
- row_counts: int32 [32], P(('dom', 'sub')), may hold values from 6 to 12
Outputs:
- remainder: float32 [384, 64, 128], P(('dom', 'sub'))
- cross_gram: float32 [64, 64], replicated
The draws below stay inside these ranges and needn't reach their ends.
Inputs may be any that keep to these rules, and one draw needn't show every extreme that they name: neighbours[p, c] is p + 1, p - 1, p + 2, p - 2 for c = 0, 1, 2, 3, or -1 where that partition is not a neighbour; slots 0 and 1 are filled wherever the partition exists; q is in p's list exactly when p is in q's.
All inputs are finite; a program needn't handle non-finite values.
Results may differ from the reference program's by a relative error of at most 0.0053.
Values may be sent and summed in bfloat16 or wider, within the bound.
No kernel may reach another device: no remote copies, remote signals or barrier semaphores. Data moves between devices by JAX's collectives and lax.ppermute only.
A program may use at most 128 MiB of HBM per device.

```python
import math
import jax
import jax.numpy as jnp
from jax import lax

DIRS = 64
TILE = 128
BLK_DEV = 12
TILES_ROW = 27
NEIGH = 4
SLOTS = 2
ITERS = 2
NBLK = 384
NPART = 32
LOCAL = 80
N_DOM = 8
N_SUB = 4


def draw_neighbours(key, part):
    key = jax.random.fold_in(key, 11)
    index = jnp.arange(N_DOM, dtype=jnp.int32)
    far_bond = jax.random.randint(key, (N_DOM,), 0, 2)
    below_bond = jnp.roll(far_bond, 2)
    upper_one = jnp.where(index + 1 < N_DOM, index + 1, -1)
    lower_one = jnp.where(index - 1 >= 0, index - 1, -1)
    upper_two = jnp.where((index + 2 < N_DOM) & (far_bond == 1), index + 2, -1)
    lower_two = jnp.where((index - 2 >= 0) & (below_bond == 1), index - 2, -1)
    return jnp.stack([upper_one, lower_one, upper_two, lower_two], axis=1).astype(jnp.int32)


def touch_ends(result, stream_key, least, top_value):
    longest = result.shape.index(max(result.shape))
    spots = []
    for shift in (0, 1):
        where = [jax.random.randint(jax.random.fold_in(stream_key, axis), (), 0, length) for axis, length in enumerate(result.shape)]
        where[longest] = (where[longest] + shift) % result.shape[longest]
        spots.append(tuple(where))
    return result.at[spots[0]].set(least).at[spots[1]].set(top_value)


def steps_of(own_key, dims, cuts, least, high):
    gain, own = 1.0, jax.random.fold_in(own_key, 6)
    for position, parts in cuts:
        steps = jnp.exp(jax.random.uniform(jax.random.fold_in(own, position), (parts,), jnp.float32, least / len(cuts), high / len(cuts)))
        gain = gain * jnp.repeat(steps, dims[position] // parts).reshape([-1 if axis == position else 1 for axis in range(len(dims))])
    return gain


def scatter_about(key, extent, deviation, bound, shards=(), held_as=jnp.bfloat16):
    result = deviation * jax.random.normal(key, extent, jnp.float32)
    if shards:
        result = result * steps_of(key, extent, shards, -0.22, 0.18)
    return jnp.clip(result, -bound, bound).astype(held_as)


def setup_inputs(seed: int = 0) -> dict:
    streams_of = jax.random.split(jax.random.key(seed), 9)
    return {
        "directions": scatter_about(streams_of[0], (NBLK, DIRS, TILE), 1.0, 6.0, ((0, 32),)),
        "tiles": scatter_about(streams_of[1], (NBLK, TILES_ROW, TILE, TILE), (TILES_ROW * TILE) ** -0.5, 0.109375, ((0, 32),)),
        "tile_cols": touch_ends(jax.random.randint(streams_of[2], (NBLK, TILES_ROW), 0, LOCAL), jax.random.fold_in(streams_of[2], 1), 0, LOCAL - 1).astype(jnp.int32),
        "friction": jnp.clip(jnp.exp(math.log(3.0) - 2.3025851 * jax.random.uniform(streams_of[3], (NBLK, TILE), jnp.float32) ** steps_of(streams_of[3], (NBLK, TILE), ((0, 32),), -0.2, 0.2)), 0.3, 3.0),
        "neighbours": draw_neighbours(jax.random.fold_in(streams_of[8], 71), 0),
        "send_idx": touch_ends(jax.random.randint(streams_of[5], (NPART, NEIGH, SLOTS), 0, BLK_DEV), jax.random.fold_in(streams_of[5], 1), 0, BLK_DEV - 1).astype(jnp.int32),
        "send_count": touch_ends(jax.random.randint(streams_of[6], (NPART, NEIGH), 1, SLOTS + 1), jax.random.fold_in(streams_of[6], 1), 1, SLOTS).astype(jnp.int32),
        "row_counts": touch_ends(jax.random.randint(streams_of[7], (NPART,), BLK_DEV // 2, BLK_DEV + 1), jax.random.fold_in(streams_of[7], 1), BLK_DEV // 2, BLK_DEV).astype(jnp.int32),
    }


def column_map(neighbours, send_idx, send_count):
    ndev = N_DOM * N_SUB
    own_count = N_SUB * BLK_DEV
    local_count = own_count + N_SUB * NEIGH * SLOTS
    device = jnp.arange(ndev, dtype=jnp.int32)[:, None]
    partition = device // N_SUB
    column = jnp.arange(local_count, dtype=jnp.int32)[None, :]
    own_global = partition * own_count + column
    offset = jnp.maximum(column - own_count, 0)
    sub_source = offset // (NEIGH * SLOTS)
    colour = offset // SLOTS % NEIGH
    slot_index = offset % SLOTS
    source = neighbours[partition, colour]
    sender = jnp.maximum(source, 0) * N_SUB + sub_source
    sent_colour = jnp.bitwise_xor(colour, 1)
    count = send_count[sender, sent_colour]
    block = send_idx[sender, sent_colour, slot_index]
    halo_global = sender * BLK_DEV + block
    halo_ok = (source >= 0) & (slot_index < count)
    is_own = column < own_count
    global_index = jnp.where(is_own, own_global, halo_global).astype(jnp.int32)
    valid = (is_own | halo_ok).astype(jnp.float32)
    return (global_index, valid)

def reference(directions, tiles, tile_cols, friction, neighbours, send_idx, send_count, row_counts):
    ndev = N_DOM * N_SUB
    global_index, valid = column_map(neighbours, send_idx, send_count)
    owner = jnp.arange(NBLK, dtype=jnp.int32) // BLK_DEV
    live = (jnp.arange(NBLK, dtype=jnp.int32) % BLK_DEV < row_counts[owner]).astype(jnp.float32)
    gcol = global_index[owner[:, None], tile_cols]
    gval = valid[owner[:, None], tile_cols]
    tiles_dev = tiles.reshape(ndev, BLK_DEV, TILES_ROW, TILE, TILE)
    gcol_dev = gcol.reshape(ndev, BLK_DEV, TILES_ROW)
    gval_dev = gval.reshape(ndev, BLK_DEV, TILES_ROW)
    high = lax.Precision.HIGHEST
    basis = directions * live[:, None, None].astype(jnp.bfloat16)
    remainder = jnp.zeros((NBLK, DIRS, TILE), jnp.float32)
    cross = jnp.zeros((DIRS, DIRS), jnp.float32)
    for step in range(ITERS):
        current = basis

        def forward_one(inputs):
            tile_set, cols, weights = inputs
            picked = current[cols].astype(jnp.float32) * weights[:, :, None, None]
            return jnp.einsum('rjkb,rjab->rka', picked, tile_set.astype(jnp.float32))
        state = lax.map(forward_one, (tiles_dev, gcol_dev, gval_dev)).reshape(NBLK, DIRS, TILE)
        weighted = (live[:, None, None] * friction[:, None, :] * state).astype(jnp.bfloat16)
        weighted_dev = weighted.reshape(ndev, BLK_DEV, DIRS, TILE)

        def adjoint_one(total, inputs):
            tile_set, cols, weights, rows = inputs
            contrib = jnp.einsum('rka,rjab->rjkb', rows.astype(jnp.float32), tile_set.astype(jnp.float32))
            contrib = contrib * weights[:, :, None, None]
            total = total.at[cols.reshape(-1)].add(contrib.reshape(-1, DIRS, TILE))
            return (total, None)
        response, unused = lax.scan(adjoint_one, jnp.zeros((NBLK, DIRS, TILE), jnp.float32), (tiles_dev, gcol_dev, gval_dev, weighted_dev))
        widened = basis.astype(jnp.float32)
        image = live[:, None, None] * (response + 1.0 * widened)
        gram = jnp.einsum('rkb,rlb->kl', widened, widened, precision=high)
        cross = jnp.einsum('rkb,rlb->kl', widened, image, precision=high)
        factor = jnp.linalg.cholesky(gram)
        coupling = jax.scipy.linalg.cho_solve((factor, True), cross)
        remainder = image - jnp.einsum('rkb,kl->rlb', widened, coupling, precision=high)
        basis = remainder.astype(jnp.bfloat16)
    return (remainder, cross)
```

```python
import functools

import jax
import jax.numpy as jnp
from jax import lax
from jax.experimental import pallas as pl
from jax.experimental.pallas import tpu as pltpu
from jax.sharding import PartitionSpec as P

ITERS = 2
F32 = jnp.float32
BF16 = jnp.bfloat16
NT = (((1,), (1,)), ((), ()))
VMEM = pl.BlockSpec(memory_space=pltpu.VMEM)
SMEM = pl.BlockSpec(memory_space=pltpu.SMEM)


def bits_of(count):
    return [1 << b for b in reversed(range(count.bit_length() - 1))]


def swap(x, axis, bit):
    peers = lax.axis_size(axis)
    return lax.ppermute(x, axis, [(i, i ^ bit) for i in range(peers)])


def swap_pairs(x, by, lower):
    peers = lax.axis_size("dom")
    low = [p for p in range(peers - by) if lower(p)]
    return lax.ppermute(x, "dom", [(p, p + by) for p in low] + [(p + by, p) for p in low])


PAIRINGS = (
    (1, lambda p: p % 2 == 0),
    (1, lambda p: p % 2 == 1),
    (2, lambda p: p % 4 < 2),
    (2, lambda p: p % 4 >= 2),
)


def split_bf16(x, pieces):
    out = []
    for _ in range(pieces):
        out.append(x.astype(BF16))
        x = x - out[-1].astype(F32)
    return out


def forward_adjoint(n_parts, cols, tiles, weight, *refs):
    parts = refs[:n_parts]
    own_keep, own_send, halo_keep, halo_send, grams, columns, held, total = refs[n_parts:]
    blocks, tiles_row, width = tiles.shape[0], tiles.shape[1], tiles.shape[2]
    dirs = grams.shape[0]
    place = 0
    for part in parts:
        for i in range(part.shape[0]):
            columns[place + i] = part[i]
        place += part.shape[0]
    total[...] = jnp.zeros_like(total)
    mine = jnp.concatenate([parts[0][i] for i in range(blocks)], axis=1)
    basis_gram = lax.dot_general(mine, mine, NT, preferred_element_type=F32)
    grams[:, :dirs] = basis_gram
    grams[:, dirs:] = basis_gram

    def forward(row):
        picked = jnp.concatenate([columns[cols[row, j]] for j in range(tiles_row)], axis=1)
        wide = jnp.concatenate([tiles[row, j] for j in range(tiles_row)], axis=1)
        state = lax.dot_general(wide, picked, NT, preferred_element_type=F32).T
        weighted = (weight[pl.ds(row, 1), :] * state).astype(BF16)
        pieces = split_bf16(state, 2)
        grams[:, dirs:] += lax.dot_general(
            jnp.concatenate(pieces, axis=1),
            jnp.concatenate([weighted] * 2, axis=1),
            NT,
            preferred_element_type=F32,
        )
        return weighted

    def adjoint(row, weighted):
        for j in range(0, tiles_row, 2):
            pair = list(range(j, min(j + 2, tiles_row)))
            wide = jnp.concatenate([tiles[row, i] for i in pair], axis=1)
            product = jnp.dot(weighted, wide, preferred_element_type=F32)
            for k, i in enumerate(pair):
                total[cols[row, i]] += product[:, k * width : (k + 1) * width]

    held[0] = forward(0)

    def step(row, carry):
        adjoint(row, held[row % 2])
        held[(row + 1) % 2] = forward(row + 1)
        return carry

    lax.fori_loop(0, blocks - 1, step, 0)
    adjoint(blocks - 1, held[(blocks - 1) % 2])
    place = 0
    for out in (own_keep, own_send, halo_keep, halo_send):
        for i in range(out.shape[0]):
            out[i] = total[place + i]
        place += out.shape[0]


def call_forward_adjoint(cols, tiles, weight, parts):
    blocks, tiles_row, width = tiles.shape[0], tiles.shape[1], tiles.shape[2]
    dirs = parts[0].shape[1]
    n = len(parts)
    own = sum(p.shape[0] for p in parts[: n // 2])
    halo = sum(p.shape[0] for p in parts[n // 2 :])
    block = lambda count: jax.ShapeDtypeStruct((count, dirs, width), F32)
    return pl.pallas_call(
        functools.partial(forward_adjoint, n),
        in_specs=[SMEM] + [VMEM] * (2 + n),
        out_specs=[VMEM] * 5,
        out_shape=[
            block(own // 2),
            block(own // 2),
            block(halo // 2),
            block(halo // 2),
            jax.ShapeDtypeStruct((dirs, 2 * dirs), F32),
        ],
        scratch_shapes=[
            pltpu.VMEM((own + halo, dirs, width), BF16),
            pltpu.VMEM((2, dirs, width), BF16),
            pltpu.VMEM((own + halo, dirs, width), F32),
        ],
        compiler_params=pltpu.CompilerParams(vmem_limit_bytes=36 << 20),
        cost_estimate=pl.CostEstimate(
            flops=4 * blocks * tiles_row * width * width * dirs,
            bytes_accessed=blocks * tiles_row * width * width * 2,
            transcendentals=0,
        ),
        name="forward_adjoint",
    )(cols, tiles, weight, *parts)


def solve(grams, coupling):
    dirs = grams.shape[0]
    m = grams[...]
    rows = lax.broadcasted_iota(jnp.int32, m.shape, 0)
    for k in range(dirs):
        row = m[k : k + 1, :] / m[k : k + 1, k : k + 1]
        m = jnp.where(rows == k, row, m - m[:, k : k + 1] * row)
    turned = m[:, dirs:].T
    coupling[...] = jnp.concatenate(split_bf16(turned, 3), axis=1)


def call_solve(grams):
    dirs = grams.shape[0]
    return pl.pallas_call(
        solve,
        in_specs=[VMEM],
        out_specs=VMEM,
        out_shape=jax.ShapeDtypeStruct((dirs, 3 * dirs), BF16),
        cost_estimate=pl.CostEstimate(flops=4 * dirs**3, bytes_accessed=12 * dirs * dirs, transcendentals=dirs),
        name="solve",
    )(grams)


def project(sends, send_mask, live, coupling, basis, keep, core, far, *refs):
    returned = refs[:4]
    remainder, next_basis, outgoing = refs[4:]
    blocks = basis.shape[0]
    slots = returned[0].shape[0]
    for b in range(blocks):
        remainder[b] = keep[b] + core[b] + far[b].astype(F32)
    for i, pieces in enumerate(returned):
        for s in range(slots):
            remainder[sends[i, s]] += pieces[s] * send_mask[i, s]
    for b in range(blocks):
        block = basis[b]
        image = live[b] * (remainder[b] + 1.0 * block.astype(F32))
        tall = jnp.concatenate([block] * 3, axis=0)
        rest = image - jnp.dot(coupling[...], tall, preferred_element_type=F32)
        remainder[b] = rest
        next_basis[b] = rest.astype(BF16)
    for i in range(4):
        for s in range(slots):
            outgoing[i * slots + s] = next_basis[sends[i, s]] * send_mask[i, s].astype(BF16)


def call_project(sends, send_mask, live, coupling, basis, keep, core, far, returned):
    blocks, dirs, width = basis.shape
    slots = returned[0].shape[0]
    return pl.pallas_call(
        project,
        in_specs=[SMEM] * 3 + [VMEM] * (5 + 4),
        out_specs=[VMEM] * 3,
        out_shape=[
            jax.ShapeDtypeStruct((blocks, dirs, width), F32),
            jax.ShapeDtypeStruct((blocks, dirs, width), BF16),
            jax.ShapeDtypeStruct((4 * slots, dirs, width), BF16),
        ],
        cost_estimate=pl.CostEstimate(
            flops=6 * blocks * dirs * dirs * width, bytes_accessed=20 * blocks * dirs * width, transcendentals=0
        ),
        name="project",
    )(sends, send_mask, live, coupling, basis, keep, core, far, *returned)


def on_device(directions, tiles, tile_cols, friction, neighbours, send_idx, send_count, row_counts):
    dom_count, sub_count = lax.axis_size("dom"), lax.axis_size("sub")
    blocks, dirs, width = directions.shape
    slots = send_idx.shape[2]
    neigh = send_idx.shape[1]
    part, me = lax.axis_index("dom"), lax.axis_index("sub")
    sub_bits, dom_bits = bits_of(sub_count), bits_of(dom_count)

    live = (jnp.arange(blocks) < row_counts[0]).astype(F32)
    odd, upper = part % 2, (part // 2) % 2
    order = jnp.stack([odd, 1 - odd, 2 + upper, 3 - upper])
    sends = send_idx[0][order]
    held = (neighbours[0] >= 0)[:, None] & (jnp.arange(slots)[None, :] < send_count[0][:, None])
    send_mask = held.astype(F32)[order]

    def place_of(sub):
        relative = jnp.bitwise_xor(sub, me)
        place = 0
        for i, bit in enumerate(sub_bits):
            place = place + jnp.where(jnp.bitwise_and(relative, bit) != 0, 1 << i, 0)
        return place

    own_columns = sub_count * blocks
    h = tile_cols - own_columns
    colour = (h // slots) % neigh
    pairing = jnp.where(colour < 2, jnp.bitwise_xor(colour, odd), jnp.bitwise_xor(colour, upper))
    halo_place = own_columns + place_of(h // (neigh * slots)) * neigh * slots + pairing * slots + h % slots
    own_place = place_of(tile_cols // blocks) * blocks + tile_cols % blocks
    cols = jnp.where(h < 0, own_place, halo_place).astype(jnp.int32)
    weight = live[:, None] * friction

    basis = directions * live[:, None, None].astype(BF16)
    outgoing = basis[sends.reshape(-1)] * send_mask.reshape(-1)[:, None, None].astype(BF16)
    remainder = None
    cross = None
    for step in range(ITERS):
        halo = [
            swap_pairs(outgoing[i * slots : (i + 1) * slots], by, lower)
            for i, (by, lower) in enumerate(PAIRINGS)
        ]
        own_parts, halo_parts = [basis], [jnp.concatenate(halo, axis=0)]
        for bit in sub_bits:
            own_parts = own_parts + [swap(x, "sub", bit) for x in own_parts]
            halo_parts = halo_parts + [swap(x, "sub", bit) for x in halo_parts]
        own_keep, own_send, halo_keep, halo_send, grams = call_forward_adjoint(
            cols, tiles, weight, own_parts + halo_parts
        )
        own_got = swap(own_send, "sub", sub_bits[-1])
        halo_got = swap(halo_send, "sub", sub_bits[-1])
        per = neigh * slots
        halo_far = swap((halo_keep[per:] + halo_got[per:]).astype(BF16), "sub", sub_bits[0])
        own_far = swap((own_keep[blocks:] + own_got[blocks:]).astype(BF16), "sub", sub_bits[0])
        back = halo_keep[:per] + halo_got[:per] + halo_far.astype(F32)
        returned = [
            swap_pairs(back[i * slots : (i + 1) * slots], by, lower)
            for i, (by, lower) in enumerate(PAIRINGS)
        ]
        for bit in reversed(sub_bits):
            grams = grams + swap(grams, "sub", bit)
        for bit in reversed(dom_bits):
            grams = grams + swap(grams, "dom", bit)
        cross = grams[:, dirs:]
        coupling = call_solve(grams)
        remainder, basis, outgoing = call_project(
            sends, send_mask, live, coupling, basis, own_keep[:blocks], own_got[:blocks], own_far, returned
        )
    return (remainder, cross)


def solution(mesh):
    in_specs = (
        P(("dom", "sub"), None, None),
        P(("dom", "sub"), None, None, None),
        P(("dom", "sub"), None),
        P(("dom", "sub"), None),
        P("dom", None),
        P(("dom", "sub"), None, None),
        P(("dom", "sub"), None),
        P(("dom", "sub")),
    )
    out_specs = (P(("dom", "sub"), None, None), P())
    return jax.shard_map(
        on_device, mesh=mesh, in_specs=in_specs, out_specs=out_specs, check_vma=False
    )
```

```python
import functools

import jax
import jax.numpy as jnp
from jax import lax
from jax.experimental import pallas as pl
from jax.experimental.pallas import tpu as pltpu
from jax.sharding import PartitionSpec as P

ITERS = 2
F32 = jnp.float32
BF16 = jnp.bfloat16
NT = (((1,), (1,)), ((), ()))
VMEM = pl.BlockSpec(memory_space=pltpu.VMEM)
SMEM = pl.BlockSpec(memory_space=pltpu.SMEM)
SMALL = pltpu.CompilerParams(vmem_limit_bytes=8 << 20)

PAIRINGS = (
    (1, lambda p: p % 2 == 0),
    (1, lambda p: p % 2 == 1),
    (2, lambda p: p % 4 < 2),
    (2, lambda p: p % 4 >= 2),
)


def bits_of(count):
    return [1 << b for b in range(count.bit_length() - 1)]


def swap(x, axis, bit):
    peers = lax.axis_size(axis)
    return lax.ppermute(x, axis, [(i, i ^ bit) for i in range(peers)])


def pair_up(x, pairing):
    by, lower = PAIRINGS[pairing]
    low = [p for p in range(lax.axis_size("dom") - by) if lower(p)]
    return lax.ppermute(x, "dom", [(p, p + by) for p in low] + [(p + by, p) for p in low])


def split_bf16(x, pieces):
    out = []
    for _ in range(pieces):
        out.append(x.astype(BF16))
        x = x - out[-1].astype(F32)
    return out


class Facts:
    def __init__(self, ref, neigh, slots):
        self.ref, self.neigh, self.slots = ref, neigh, slots

    def part(self):
        return self.ref[0]

    def sub(self):
        return self.ref[1]

    def live_rows(self):
        return self.ref[2]

    def live(self, block):
        return (block < self.live_rows()).astype(F32)

    def colour(self, pairing):
        odd, upper = self.part() % 2, (self.part() // 2) % 2
        return (odd, 1 - odd, 2 + upper, 3 - upper)[pairing]

    def send(self, pairing, slot):
        colour = self.colour(pairing)
        sent = (self.ref[3 + colour] >= 0) & (slot < self.ref[3 + self.neigh + colour])
        return self.ref[3 + 2 * self.neigh + colour * self.slots + slot], sent.astype(F32)


def pack_facts(neighbours, send_idx, send_count, row_counts):
    place = jnp.stack([lax.axis_index("dom"), lax.axis_index("sub")]).astype(jnp.int32)
    return jnp.concatenate(
        [place, row_counts, neighbours.reshape(-1), send_count.reshape(-1), send_idx.reshape(-1)]
    )


def write_outgoing(facts, basis, outgoing):
    for pairing, out in enumerate(outgoing):
        for slot in range(facts.slots):
            block, sent = facts.send(pairing, slot)
            out[slot] = basis[block] * sent.astype(BF16)


def prepare(shape, facts, directions, basis, *outgoing):
    facts = Facts(facts, *shape)
    for b in range(basis.shape[0]):
        basis[b] = directions[b] * facts.live(b).astype(BF16)
    write_outgoing(facts, basis, outgoing)


def call_prepare(shape, facts, directions):
    out = jax.ShapeDtypeStruct((shape[1],) + directions.shape[1:], BF16)
    return pl.pallas_call(
        functools.partial(prepare, shape),
        in_specs=[SMEM, VMEM],
        out_specs=[VMEM] * 5,
        out_shape=[jax.ShapeDtypeStruct(directions.shape, BF16)] + [out] * 4,
        compiler_params=SMALL,
        name="prepare",
    )(facts, directions)


def forward_adjoint(shape, relatives, facts, cols, tiles, friction, *refs):
    neigh, slots = shape
    count = len(relatives)
    own_parts, halo_parts = refs[:count], refs[count : 2 * count]
    keep, send, columns, total, held = refs[2 * count :]
    facts = Facts(facts, neigh, slots)
    blocks, tiles_row, width = tiles.shape[0], tiles.shape[1], tiles.shape[2]
    dirs = keep.shape[1]
    live_rows = facts.live_rows()

    own_base = [jnp.bitwise_xor(facts.sub(), r) * blocks for r in relatives]
    halo_base = [
        [
            count * blocks + (jnp.bitwise_xor(facts.sub(), r) * neigh + facts.colour(i)) * slots
            for i in range(neigh)
        ]
        for r in relatives
    ]
    for part, base in zip(own_parts, own_base):
        for i in range(blocks):
            columns[base + i] = part[i]
    for part, bases in zip(halo_parts, halo_base):
        for i in range(neigh):
            for s in range(slots):
                columns[bases[i] + s] = part[i * slots + s]
    total[...] = jnp.zeros_like(total)
    mine = jnp.concatenate([own_parts[0][i] for i in range(blocks)], axis=1)
    basis_gram = lax.dot_general(mine, mine, NT, preferred_element_type=F32)
    grams = send.at[send.shape[0] - 1]
    grams[:, :dirs] = basis_gram
    grams[:, dirs:] = basis_gram

    def forward(row):
        picked = jnp.concatenate([columns[cols[row, j]] for j in range(tiles_row)], axis=1)
        wide = jnp.concatenate([tiles[row, j] for j in range(tiles_row)], axis=1)
        state = lax.dot_general(wide, picked, NT, preferred_element_type=F32).T
        weighted = (friction[pl.ds(row, 1), :] * state).astype(BF16)
        grams[:, dirs:] += lax.dot_general(
            jnp.concatenate(split_bf16(state, 2), axis=1),
            jnp.concatenate([weighted] * 2, axis=1),
            NT,
            preferred_element_type=F32,
        )
        return weighted

    def adjoint(row, weighted):
        for j in range(0, tiles_row, 2):
            pair = list(range(j, min(j + 2, tiles_row)))
            wide = jnp.concatenate([tiles[row, i] for i in pair], axis=1)
            product = jnp.dot(weighted, wide, preferred_element_type=F32)
            for k, i in enumerate(pair):
                total[cols[row, i]] += product[:, k * width : (k + 1) * width]

    def step(row, carry):
        adjoint(row, held[row % 2])
        held[(row + 1) % 2] = forward(row + 1)
        return carry

    held[0] = forward(0)
    lax.fori_loop(0, live_rows - 1, step, 0)
    adjoint(live_rows - 1, held[(live_rows - 1) % 2])

    half = count // 2
    for out, chosen in ((keep, range(half)), (send, range(half, count))):
        place = 0
        for k in chosen:
            for i in range(blocks):
                out[place + i] = total[own_base[k] + i]
            place += blocks
        for k in chosen:
            for i in range(neigh):
                for s in range(slots):
                    out[place + i * slots + s] = total[halo_base[k][i] + s]
            place += neigh * slots


def call_forward_adjoint(shape, relatives, facts, cols, tiles, friction, own_parts, halo_parts):
    blocks, tiles_row, width = tiles.shape[0], tiles.shape[1], tiles.shape[2]
    dirs = own_parts[0].shape[1]
    count = len(relatives)
    local = count * (blocks + shape[0] * shape[1])
    return pl.pallas_call(
        functools.partial(forward_adjoint, shape, relatives),
        in_specs=[SMEM, SMEM, VMEM, VMEM] + [VMEM] * (2 * count),
        out_specs=[VMEM] * 2,
        out_shape=[
            jax.ShapeDtypeStruct((local // 2, dirs, width), F32),
            jax.ShapeDtypeStruct((local // 2 + 1, dirs, width), F32),
        ],
        scratch_shapes=[
            pltpu.VMEM((local, dirs, width), BF16),
            pltpu.VMEM((local, dirs, width), F32),
            pltpu.VMEM((2, dirs, width), BF16),
        ],
        compiler_params=pltpu.CompilerParams(vmem_limit_bytes=24 << 20),
        cost_estimate=pl.CostEstimate(
            flops=4 * blocks * tiles_row * width * width * dirs,
            bytes_accessed=blocks * tiles_row * width * width * 2,
            transcendentals=0,
        ),
        name="forward_adjoint",
    )(facts, cols, tiles, friction, *own_parts, *halo_parts)


def join(blocks, halo, keep, send, got, near_own, near_halo, far_own, far_halo):
    for b in range(blocks):
        near_own[b] = keep[b] + got[b]
        far_own[b] = (keep[blocks + b] + got[blocks + b]).astype(BF16)
    for h in range(halo):
        near_halo[h] = keep[2 * blocks + h] + got[2 * blocks + h]
        far_halo[h] = (keep[2 * blocks + halo + h] + got[2 * blocks + halo + h]).astype(BF16)
    last = send.shape[0] - 1
    for i, piece in enumerate(split_bf16(send[last] + got[last], 3)):
        far_halo[halo + i] = piece


def call_join(blocks, halo, keep, send, got):
    tail = keep.shape[1:]
    return pl.pallas_call(
        functools.partial(join, blocks, halo),
        in_specs=[VMEM] * 3,
        out_specs=[VMEM] * 4,
        out_shape=[
            jax.ShapeDtypeStruct((blocks,) + tail, F32),
            jax.ShapeDtypeStruct((halo,) + tail, F32),
            jax.ShapeDtypeStruct((blocks,) + tail, BF16),
            jax.ShapeDtypeStruct((halo + 3,) + tail, BF16),
        ],
        compiler_params=SMALL,
        name="join",
    )(keep, send, got)


def hand_back(slots, near_halo, sent, got, *outs):
    halo = near_halo.shape[0]
    grams = [sum(x[halo + i].astype(F32) for i in reversed(range(3))) for x in (sent, got)]
    for pairing, out in enumerate(outs):
        for s in range(slots):
            out[s] = near_halo[pairing * slots + s] + got[pairing * slots + s].astype(F32)
    outs[0][slots] = grams[0] + grams[1]


def call_hand_back(slots, near_halo, sent, got):
    tail = near_halo.shape[1:]
    out = lambda n: jax.ShapeDtypeStruct((n,) + tail, F32)
    return pl.pallas_call(
        functools.partial(hand_back, slots),
        in_specs=[VMEM] * 3,
        out_specs=[VMEM] * 4,
        out_shape=[out(slots + 1), out(slots), out(slots), out(slots)],
        compiler_params=SMALL,
        name="hand_back",
    )(near_halo, sent, got)


def eliminate(grams, dirs):
    wide = grams.shape[1]
    panels = [grams[8 * i : 8 * i + 8, :] for i in range(dirs // 8)]
    rows = lax.broadcasted_iota(jnp.int32, (8, wide), 0)

    def spread(x, column):
        return jnp.broadcast_to(x[:, column : column + 1], (8, wide))

    for k in range(dirs // 8):
        pivot = panels[k]
        lead = [spread(pivot, 8 * k + j) for j in range(8)]
        for t in range(8):
            inverse = 1.0 / lead[t][t : t + 1, :]
            row = pivot[t : t + 1, :] * inverse
            pivot = jnp.where(rows == t, row, pivot - lead[t] * row)
            for j in range(t + 1, 8):
                other = lead[j][t : t + 1, :] * inverse
                lead[j] = jnp.where(rows == t, other, lead[j] - lead[t] * other)
        for i in range(dirs // 8):
            if i != k:
                old = panels[i]
                new = old
                for j in range(8):
                    new = new - spread(old, 8 * k + j) * pivot[j : j + 1, :]
                panels[i] = new
        panels[k] = pivot
    return jnp.concatenate(panels, axis=0)[:, dirs:]


def project(shape, last, facts, grams_here, grams_there, basis, near_own, far_own, *refs):
    slots = shape[1]
    facts = Facts(facts, *shape)
    returned, outs, image = refs[:4], refs[4:-1], refs[-1]
    blocks, dirs = basis.shape[0], basis.shape[1]
    for b in range(blocks):
        image[b] = near_own[b] + far_own[b].astype(F32)
    for pairing, back in enumerate(returned):
        for s in range(slots):
            block, sent = facts.send(pairing, s)
            image[block] += back[s] * sent
    grams = grams_here[...] + grams_there[...]
    coupling = eliminate(grams, dirs)
    turned = jnp.concatenate(split_bf16(coupling.T, 3), axis=1)
    if last:
        outs[1][...] = grams[:, dirs:]
    for b in range(blocks):
        block = basis[b]
        wanted = facts.live(b) * (image[b] + 1.0 * block.astype(F32))
        tall = jnp.concatenate([block] * 3, axis=0)
        rest = wanted - jnp.dot(turned, tall, preferred_element_type=F32)
        outs[0][b] = rest.astype(outs[0].dtype)
    if not last:
        write_outgoing(facts, outs[0], outs[1:])


def call_project(shape, last, facts, grams_here, grams_there, basis, near_own, far_own, returned):
    blocks, dirs, width = basis.shape
    if last:
        out_shape = [jax.ShapeDtypeStruct(basis.shape, F32), jax.ShapeDtypeStruct((dirs, dirs), F32)]
    else:
        out_shape = [jax.ShapeDtypeStruct(basis.shape, BF16)]
        out_shape += [jax.ShapeDtypeStruct((shape[1], dirs, width), BF16)] * 4
    return pl.pallas_call(
        functools.partial(project, shape, last),
        in_specs=[SMEM] + [VMEM] * 9,
        out_specs=[VMEM] * len(out_shape),
        out_shape=out_shape,
        scratch_shapes=[pltpu.VMEM((blocks, dirs, width), F32)],
        cost_estimate=pl.CostEstimate(
            flops=6 * blocks * dirs * dirs * width, bytes_accessed=20 * blocks * dirs * width, transcendentals=0
        ),
        compiler_params=SMALL,
        name="project",
    )(facts, grams_here, grams_there, basis, near_own, far_own, *returned)


def on_device(directions, tiles, tile_cols, friction, neighbours, send_idx, send_count, row_counts):
    near, far = bits_of(lax.axis_size("sub"))
    dom_bits = bits_of(lax.axis_size("dom"))
    blocks = directions.shape[0]
    neigh, slots = send_idx.shape[1:]
    shape = (neigh, slots)
    relatives = (0, far, near, near | far)
    facts = pack_facts(neighbours, send_idx, send_count, row_counts)
    basis, *outgoing = call_prepare(shape, facts, directions)
    for step in range(ITERS):
        own_far = swap(basis, "sub", far)
        halo = jnp.concatenate([pair_up(x, i) for i, x in enumerate(outgoing)], axis=0)
        halo_far = swap(halo, "sub", far)
        own_parts = [basis, own_far, swap(basis, "sub", near), swap(own_far, "sub", near)]
        halo_parts = [halo, halo_far, swap(halo, "sub", near), swap(halo_far, "sub", near)]
        keep, send = call_forward_adjoint(
            shape, relatives, facts, tile_cols, tiles, friction, own_parts, halo_parts
        )
        got = swap(send, "sub", near)
        near_own, near_halo, far_own, far_halo = call_join(blocks, neigh * slots, keep, send, got)
        far_halo_got = swap(far_halo, "sub", far)
        far_own_got = swap(far_own, "sub", far)
        back = call_hand_back(slots, near_halo, far_halo, far_halo_got)
        first = pair_up(back[0], 0)
        third = jnp.concatenate([back[2], back[0][slots:] + first[slots:]], axis=0)
        third_got = pair_up(third, 2)
        returned = [first, pair_up(back[1], 1), third_got, pair_up(back[3], 3)]
        here, there = third[slots], third_got[slots]
        for bit in dom_bits[2:]:
            here = here + there
            there = swap(here, "dom", bit)
        last = step == ITERS - 1
        basis, *outgoing = call_project(
            shape, last, facts, here, there, basis, near_own, far_own_got, returned
        )
    remainder, cross = basis, outgoing[0]
    return (remainder, cross)


def solution(mesh):
    in_specs = (
        P(("dom", "sub"), None, None),
        P(("dom", "sub"), None, None, None),
        P(("dom", "sub"), None),
        P(("dom", "sub"), None),
        P("dom", None),
        P(("dom", "sub"), None, None),
        P(("dom", "sub"), None),
        P(("dom", "sub")),
    )
    out_specs = (P(("dom", "sub"), None, None), P())
    return jax.shard_map(
        on_device, mesh=mesh, in_specs=in_specs, out_specs=out_specs, check_vma=False
    )
```

```python
import functools

import jax
import jax.numpy as jnp
from jax import lax
from jax.experimental import pallas as pl
from jax.experimental.pallas import tpu as pltpu
from jax.sharding import PartitionSpec as P

ITERS = 2
F32 = jnp.float32
BF16 = jnp.bfloat16
NT = (((1,), (1,)), ((), ()))
VMEM = pl.BlockSpec(memory_space=pltpu.VMEM)
SMEM = pl.BlockSpec(memory_space=pltpu.SMEM)
ANY = pl.BlockSpec(memory_space=pl.ANY)
SMALL = pltpu.CompilerParams(vmem_limit_bytes=8 << 20)

PAIRINGS = (lambda p: p % 4 < 2, lambda p: p % 4 >= 2)


def bits_of(count):
    return [1 << b for b in range(count.bit_length() - 1)]


def swap(x, axis, bit):
    peers = lax.axis_size(axis)
    return lax.ppermute(x, axis, [(i, i ^ bit) for i in range(peers)])


def pair_up(x, pairing):
    low = [p for p in range(lax.axis_size("dom") - 2) if PAIRINGS[pairing](p)]
    return lax.ppermute(x, "dom", [(p, p + 2) for p in low] + [(p + 2, p) for p in low])


def split_bf16(x, pieces):
    out = []
    for _ in range(pieces):
        out.append(x.astype(BF16))
        x = x - out[-1].astype(F32)
    return out


def joined(ref, start):
    return ref[start + 2].astype(F32) + ref[start + 1].astype(F32) + ref[start].astype(F32)


class Facts:
    def __init__(self, ref, neigh, slots):
        self.ref, self.neigh, self.slots = ref, neigh, slots

    def odd(self):
        return self.ref[0, 0] % 2

    def upper(self):
        return (self.ref[0, 0] // 2) % 2

    def sub(self):
        return self.ref[0, 1]

    def live_rows(self):
        return self.ref[0, 2]

    def live(self, block):
        return (block < self.live_rows()).astype(F32)

    def colour(self, role):
        return (self.odd(), 1 - self.odd(), 2 + self.upper(), 3 - self.upper())[role]

    def relays(self, pairing, out):
        down = self.upper() if pairing == 0 else 1 - self.upper()
        return (down != self.odd() if out else down == self.odd()).astype(F32)

    def send(self, role, slot):
        colour = self.colour(role)
        sent = (self.ref[1, colour] >= 0) & (slot < self.ref[2, colour])
        return self.ref[3 + slot, colour], sent.astype(F32)


def pack_facts(neighbours, send_idx, send_count, row_counts):
    place = jnp.stack([lax.axis_index("dom"), lax.axis_index("sub")]).astype(jnp.int32)
    first = jnp.pad(jnp.concatenate([place, row_counts]), (0, neighbours.shape[1] - 3))
    return jnp.concatenate([first[None, :], neighbours, send_count, jnp.swapaxes(send_idx[0], 0, 1)])


def write_outgoing(facts, basis, flip, first, second):
    for slot in range(facts.slots):
        block, sent = facts.send(0, slot)
        flip[slot] = basis[block] * sent.astype(BF16)
        block, sent = facts.send(1, slot)
        far = basis[block] * sent.astype(BF16)
        for pairing, out in enumerate((first, second)):
            block, sent = facts.send(2 + pairing, slot)
            out[slot] = basis[block] * sent.astype(BF16)
            out[facts.slots + slot] = far * facts.relays(pairing, True).astype(BF16)


def outgoing_shapes(slots, dirs, width):
    return [jax.ShapeDtypeStruct((n * slots, dirs, width), BF16) for n in (1, 2, 2)]


def prepare(shape, facts, directions, basis, ways, *outgoing):
    facts = Facts(facts, *shape)
    for pairing in range(2):
        ways[pairing] = jnp.full(ways.shape[1:], facts.relays(pairing, False), F32).astype(BF16)
    for b in range(basis.shape[0]):
        basis[b] = directions[b] * facts.live(b).astype(BF16)
    write_outgoing(facts, basis, *outgoing)


def call_prepare(shape, facts, directions):
    return pl.pallas_call(
        functools.partial(prepare, shape),
        in_specs=[SMEM, VMEM],
        out_specs=[VMEM] * 5,
        out_shape=[
            jax.ShapeDtypeStruct(directions.shape, BF16),
            jax.ShapeDtypeStruct((2, 16, directions.shape[2]), BF16),
        ]
        + outgoing_shapes(shape[1], *directions.shape[1:]),
        compiler_params=SMALL,
        cost_estimate=pl.CostEstimate(flops=8 << 30, bytes_accessed=64 << 20, transcendentals=0),
        name="prepare",
    )(facts, directions)


def pass_on(slots, ways, flip, first, second, out):
    for s in range(slots):
        out[s] = flip[s]
        out[slots + s] = first[slots + s] * ways[0, :1] + second[slots + s] * ways[1, :1]


def call_pass_on(slots, ways, flip, first, second):
    return pl.pallas_call(
        functools.partial(pass_on, slots),
        in_specs=[VMEM] * 4,
        out_specs=VMEM,
        out_shape=jax.ShapeDtypeStruct(first.shape, BF16),
        compiler_params=SMALL,
        name="pass_on",
    )(ways, flip, first, second)


def stack(slots, flip, first, second, *refs):
    out = refs[-1]
    for s in range(2 * slots):
        out[s] = flip[s]
    for s in range(slots):
        out[2 * slots + s] = first[s]
        out[3 * slots + s] = second[s]


def call_stack(slots, flip, first, second, after):
    return pl.pallas_call(
        functools.partial(stack, slots),
        in_specs=[VMEM] * 3 + [ANY] * len(after),
        out_specs=VMEM,
        out_shape=jax.ShapeDtypeStruct((4 * slots,) + flip.shape[1:], BF16),
        compiler_params=SMALL,
        name="stack",
    )(flip, first, second, *after)


def forward_adjoint(shape, relatives, facts, cols, tiles, friction, *refs):
    neigh, slots = shape
    count = len(relatives)
    own_parts, halo_parts, refs = refs[:count], refs[count : 2 * count], refs[2 * count :]
    keep, send, grams = refs[:3]
    facts = Facts(facts, neigh, slots)
    blocks, tiles_row, width = tiles.shape[0], tiles.shape[1], tiles.shape[2]
    dirs = grams.shape[0]
    live_rows = facts.live_rows()
    columns, total, weights, pieces = refs[3:]

    own_base = [jnp.bitwise_xor(facts.sub(), r) * blocks for r in relatives]
    halo_base = [
        [
            count * blocks + (jnp.bitwise_xor(facts.sub(), r) * neigh + facts.colour(i)) * slots
            for i in range(neigh)
        ]
        for r in relatives
    ]
    for part, base in zip(own_parts, own_base):
        for i in range(blocks):
            columns[base + i] = part[i]
    for part, bases in zip(halo_parts, halo_base):
        for i in range(neigh):
            for s in range(slots):
                columns[bases[i] + s] = part[i * slots + s]
    total[...] = jnp.zeros_like(total)
    weights[...] = jnp.zeros_like(weights)
    pieces[...] = jnp.zeros_like(pieces)

    def forward(row):
        picked = jnp.concatenate([columns[cols[row, j]] for j in range(tiles_row)], axis=1)
        wide = jnp.concatenate([tiles[row, j] for j in range(tiles_row)], axis=1)
        state = lax.dot_general(wide, picked, NT, preferred_element_type=F32).T
        weights[row] = (friction[pl.ds(row, 1), :] * state).astype(BF16)
        pieces[row] = jnp.concatenate(split_bf16(state, 2), axis=1)

    def adjoint(row):
        weighted = weights[row]
        for j in range(0, tiles_row, 2):
            pair = list(range(j, min(j + 2, tiles_row)))
            wide = jnp.concatenate([tiles[row, i] for i in pair], axis=1)
            product = jnp.dot(weighted, wide, preferred_element_type=F32)
            for k, i in enumerate(pair):
                total[cols[row, i]] += product[:, k * width : (k + 1) * width]

    def step(row, carry):
        adjoint(row)
        forward(row + 1)
        return carry

    forward(0)
    lax.fori_loop(0, live_rows - 1, step, 0)
    adjoint(live_rows - 1)

    mine = jnp.concatenate([own_parts[0][i] for i in range(blocks)], axis=1)
    basis_gram = lax.dot_general(mine, mine, NT, preferred_element_type=F32)
    cross_gram = lax.dot_general(
        jnp.concatenate([pieces[i] for i in range(blocks)], axis=1),
        jnp.concatenate([weights[i // 2] for i in range(2 * blocks)], axis=1),
        NT,
        preferred_element_type=F32,
    )
    grams[:, :dirs] = basis_gram
    grams[:, dirs:] = basis_gram + cross_gram

    half = count // 2
    for out, chosen in ((keep, range(half)), (send, range(half, count))):
        place = 0
        for k in chosen:
            for i in range(blocks):
                out[place + i] = total[own_base[k] + i]
            place += blocks
        for k in chosen:
            for i in range(neigh):
                for s in range(slots):
                    out[place + i * slots + s] = total[halo_base[k][i] + s]
            place += neigh * slots


def call_forward_adjoint(shape, relatives, facts, cols, tiles, friction, own_parts, halo_parts):
    blocks, tiles_row, width = tiles.shape[0], tiles.shape[1], tiles.shape[2]
    dirs = own_parts[0].shape[1]
    count = len(relatives)
    own, halo = count * blocks, count * shape[0] * shape[1]
    out = lambda n: jax.ShapeDtypeStruct((n, dirs, width), F32)
    out_shape = [out((own + halo) // 2)] * 2 + [jax.ShapeDtypeStruct((dirs, 2 * dirs), F32)]
    scratch_shapes = [
        pltpu.VMEM((own + halo, dirs, width), BF16),
        pltpu.VMEM((own + halo, dirs, width), F32),
        pltpu.VMEM((blocks, dirs, width), BF16),
        pltpu.VMEM((blocks, dirs, 2 * width), BF16),
    ]
    return pl.pallas_call(
        functools.partial(forward_adjoint, shape, relatives),
        in_specs=[SMEM, SMEM, VMEM, VMEM] + [VMEM] * (2 * count),
        out_specs=[VMEM] * len(out_shape),
        out_shape=out_shape,
        scratch_shapes=scratch_shapes,
        compiler_params=pltpu.CompilerParams(vmem_limit_bytes=24 << 20),
        cost_estimate=pl.CostEstimate(
            flops=4 * blocks * tiles_row * width * width * dirs,
            bytes_accessed=blocks * tiles_row * width * width * 2,
            transcendentals=0,
        ),
        name="forward_adjoint",
    )(facts, cols, tiles, friction, *own_parts, *halo_parts)


def join(start, keep, got, *refs):
    near, far = refs[-2:]
    count = near.shape[0]
    for i in range(count):
        near[i] = keep[start + i] + got[start + i]
        far[i] = (keep[start + count + i] + got[start + count + i]).astype(BF16)


def call_join(start, count, keep, got, after):
    shape = (count,) + keep.shape[1:]
    return pl.pallas_call(
        functools.partial(join, start),
        in_specs=[VMEM] * 2 + [ANY] * len(after),
        out_specs=[VMEM] * 2,
        out_shape=[jax.ShapeDtypeStruct(shape, F32), jax.ShapeDtypeStruct(shape, BF16)],
        compiler_params=SMALL,
        name="join",
    )(keep, got, *after)


def hand_back(slots, near_halo, far_halo, here, there, flip, first, second):
    sums = [(near_halo[i] + far_halo[i].astype(F32)).astype(BF16) for i in range(near_halo.shape[0])]
    for s in range(2 * slots):
        flip[s] = sums[s]
    for s in range(slots):
        first[s] = sums[2 * slots + s]
        second[s] = sums[3 * slots + s]
    for i, piece in enumerate(split_bf16(here[...] + there[...], 3)):
        flip[2 * slots + i] = piece


def call_hand_back(slots, near_halo, far_halo, here, there):
    tail = near_halo.shape[1:]
    out = lambda n: jax.ShapeDtypeStruct((n,) + tail, BF16)
    return pl.pallas_call(
        functools.partial(hand_back, slots),
        in_specs=[VMEM] * 4,
        out_specs=[VMEM] * 3,
        out_shape=[out(2 * slots + 3), out(slots), out(slots)],
        compiler_params=SMALL,
        name="hand_back",
    )(near_halo, far_halo, here, there)


def pass_back(slots, ways, flip, got, first, second, first_out, second_out):
    for s in range(slots):
        first_out[s] = first[s]
        second_out[s] = second[s]
        first_out[slots + s] = got[slots + s] * ways[0, :1]
        second_out[slots + s] = got[slots + s] * ways[1, :1]
    for i, piece in enumerate(split_bf16(joined(flip, 2 * slots) + joined(got, 2 * slots), 3)):
        first_out[2 * slots + i] = piece


def call_pass_back(slots, ways, flip, got, first, second):
    tail = flip.shape[1:]
    out = lambda n: jax.ShapeDtypeStruct((n,) + tail, BF16)
    return pl.pallas_call(
        functools.partial(pass_back, slots),
        in_specs=[VMEM] * 5,
        out_specs=[VMEM] * 2,
        out_shape=[out(2 * slots + 3), out(2 * slots)],
        compiler_params=SMALL,
        name="pass_back",
    )(ways, flip, got, first, second)


def eliminate(grams, dirs):
    wide = grams.shape[1]
    panels = [grams[8 * i : 8 * i + 8, :] for i in range(dirs // 8)]
    rows = lax.broadcasted_iota(jnp.int32, (8, wide), 0)

    def spread(x, column):
        return jnp.broadcast_to(x[:, column : column + 1], (8, wide))

    for k in range(dirs // 8):
        pivot = panels[k]
        lead = [spread(pivot, 8 * k + j) for j in range(8)]
        for t in range(8):
            inverse = 1.0 / lead[t][t : t + 1, :]
            row = pivot[t : t + 1, :] * inverse
            pivot = jnp.where(rows == t, row, pivot - lead[t] * row)
            for j in range(t + 1, 8):
                other = lead[j][t : t + 1, :] * inverse
                lead[j] = jnp.where(rows == t, other, lead[j] - lead[t] * other)
        for i in range(dirs // 8):
            if i != k:
                old = panels[i]
                new = old
                for j in range(8):
                    new = new - spread(old, 8 * k + j) * pivot[j : j + 1, :]
                panels[i] = new
        panels[k] = pivot
    return jnp.concatenate(panels, axis=0)[:, dirs:]


def project(shape, last, facts, passed, basis, near_own, far_own, *refs):
    slots = shape[1]
    facts = Facts(facts, *shape)
    flip, pairs, outs, image = refs[0], refs[1:3], refs[3:-1], refs[-1]
    blocks, dirs = basis.shape[0], basis.shape[1]
    for b in range(blocks):
        image[b] = near_own[b] + far_own[b].astype(F32)
    for s in range(slots):
        relayed = sum(x[slots + s].astype(F32) * facts.relays(i, True) for i, x in enumerate(pairs))
        for role, back in enumerate((flip[s], relayed, pairs[0][s], pairs[1][s])):
            block, sent = facts.send(role, s)
            image[block] += back.astype(F32) * sent
    grams = joined(passed, 2 * slots) + joined(pairs[0], 2 * slots)
    coupling = eliminate(grams, dirs)
    turned = jnp.concatenate(split_bf16(coupling.T, 3), axis=1)
    if last:
        outs[1][...] = grams[:, dirs:]
    for b in range(blocks):
        block = basis[b]
        wanted = facts.live(b) * (image[b] + 1.0 * block.astype(F32))
        tall = jnp.concatenate([block] * 3, axis=0)
        rest = wanted - jnp.dot(turned, tall, preferred_element_type=F32)
        outs[0][b] = rest.astype(outs[0].dtype)
    if not last:
        write_outgoing(facts, outs[0], *outs[1:])


def call_project(shape, last, facts, sent, basis, near_own, far_own, returned):
    blocks, dirs, width = basis.shape
    if last:
        out_shape = [jax.ShapeDtypeStruct(basis.shape, F32), jax.ShapeDtypeStruct((dirs, dirs), F32)]
    else:
        out_shape = [jax.ShapeDtypeStruct(basis.shape, BF16)]
        out_shape += outgoing_shapes(shape[1], dirs, width)
    return pl.pallas_call(
        functools.partial(project, shape, last),
        in_specs=[SMEM] + [VMEM] * 7,
        out_specs=[VMEM] * len(out_shape),
        out_shape=out_shape,
        scratch_shapes=[pltpu.VMEM((blocks, dirs, width), F32)],
        cost_estimate=pl.CostEstimate(
            flops=6 * blocks * dirs * dirs * width, bytes_accessed=20 * blocks * dirs * width, transcendentals=0
        ),
        compiler_params=SMALL,
        name="project",
    )(facts, sent, basis, near_own, far_own, *returned)


def on_device(directions, tiles, tile_cols, friction, neighbours, send_idx, send_count, row_counts):
    near, far = bits_of(lax.axis_size("sub"))
    dom_bits = bits_of(lax.axis_size("dom"))
    blocks = directions.shape[0]
    neigh, slots = send_idx.shape[1:]
    shape = (neigh, slots)
    relatives = (0, far, near, near | far)
    facts = pack_facts(neighbours, send_idx, send_count, row_counts)
    basis, ways, *outgoing = call_prepare(shape, facts, directions)
    for step in range(ITERS):
        own_far, own_near = swap(basis, "sub", far), swap(basis, "sub", near)
        pairs = [pair_up(x, i) for i, x in enumerate(outgoing[1:])]
        flip = swap(call_pass_on(slots, ways, outgoing[0], *pairs), "dom", dom_bits[0])
        halo = call_stack(slots, flip, *pairs, [own_far, own_near])
        halo_far = swap(halo, "sub", far)
        own_parts = [basis, own_far, own_near, swap(own_far, "sub", near)]
        halo_parts = [halo, halo_far, swap(halo, "sub", near), swap(halo_far, "sub", near)]
        keep, send, grams = call_forward_adjoint(
            shape, relatives, facts, tile_cols, tiles, friction, own_parts, halo_parts
        )
        for bit in dom_bits[2:]:
            grams = grams + swap(grams, "dom", bit)
        got = swap(send, "sub", near)
        near_halo, far_halo = call_join(2 * blocks, neigh * slots, keep, got, [grams])
        far_halo = swap(far_halo, "sub", far)
        grams = grams + swap(grams, "sub", near)
        grams_got = swap(grams, "sub", far)
        near_own, far_own = call_join(0, blocks, keep, got, [grams_got])
        far_own_got = swap(far_own, "sub", far)
        flip, *back = call_hand_back(slots, near_halo, far_halo, grams, grams_got)
        flip_got = swap(flip, "dom", dom_bits[0])
        back = call_pass_back(slots, ways, flip, flip_got, *back)
        returned = [flip_got] + [pair_up(x, i) for i, x in enumerate(back)]
        last = step == ITERS - 1
        basis, *outgoing = call_project(
            shape, last, facts, back[0], basis, near_own, far_own_got, returned
        )
    remainder, cross = basis, outgoing[0]
    return (remainder, cross)


def solution(mesh):
    in_specs = (
        P(("dom", "sub"), None, None),
        P(("dom", "sub"), None, None, None),
        P(("dom", "sub"), None),
        P(("dom", "sub"), None),
        P("dom", None),
        P(("dom", "sub"), None, None),
        P(("dom", "sub"), None),
        P(("dom", "sub")),
    )
    out_specs = (P(("dom", "sub"), None, None), P())
    return jax.shard_map(
        on_device, mesh=mesh, in_specs=in_specs, out_specs=out_specs, check_vma=False
    )
```

```python
import functools

import jax
import jax.numpy as jnp
from jax import lax
from jax.experimental import pallas as pl
from jax.experimental.pallas import tpu as pltpu
from jax.sharding import PartitionSpec as P

ITERS = 2
STREAMED = 8
F32 = jnp.float32
BF16 = jnp.bfloat16
NT = (((1,), (1,)), ((), ()))
VMEM = pl.BlockSpec(memory_space=pltpu.VMEM)
SMEM = pl.BlockSpec(memory_space=pltpu.SMEM)
ANY = pl.BlockSpec(memory_space=pl.ANY)
SMALL = pltpu.CompilerParams(vmem_limit_bytes=8 << 20)

PAIRINGS = (lambda p: p % 4 < 2, lambda p: p % 4 >= 2)


def bits_of(count):
    return [1 << b for b in range(count.bit_length() - 1)]


def swap(x, axis, bit):
    peers = lax.axis_size(axis)
    return lax.ppermute(x, axis, [(i, i ^ bit) for i in range(peers)])


def swap_both(x, dom_bit, sub_bit):
    subs = lax.axis_size("sub")
    peers = [(p, s) for p in range(lax.axis_size("dom")) for s in range(subs)]
    pairs = [(p * subs + s, (p ^ dom_bit) * subs + (s ^ sub_bit)) for p, s in peers]
    return lax.ppermute(x, ("dom", "sub"), pairs)


def pair_up(x, pairing):
    low = [p for p in range(lax.axis_size("dom") - 2) if PAIRINGS[pairing](p)]
    return lax.ppermute(x, "dom", [(p, p + 2) for p in low] + [(p + 2, p) for p in low])


def split_bf16(x, pieces):
    out = []
    for _ in range(pieces):
        out.append(x.astype(BF16))
        x = x - out[-1].astype(F32)
    return out


def joined(ref, start):
    return ref[start + 1].astype(F32) + ref[start].astype(F32)


class Facts:
    def __init__(self, ref, neigh, slots):
        self.ref, self.neigh, self.slots = ref, neigh, slots

    def odd(self):
        return self.ref[0, 0] % 2

    def upper(self):
        return (self.ref[0, 0] // 2) % 2

    def sub(self):
        return self.ref[0, 1]

    def live_rows(self):
        return self.ref[0, 2]

    def live(self, block):
        return (block < self.live_rows()).astype(F32)

    def colour(self, role):
        return (self.odd(), 1 - self.odd(), 2 + self.upper(), 3 - self.upper())[role]

    def relays(self, pairing, out):
        down = self.upper() if pairing == 0 else 1 - self.upper()
        return (down != self.odd() if out else down == self.odd()).astype(F32)

    def send(self, role, slot):
        colour = self.colour(role)
        sent = (self.ref[1, colour] >= 0) & (slot < self.ref[2, colour])
        return self.ref[3 + slot, colour], sent.astype(F32)


def pack_facts(neighbours, send_idx, send_count, row_counts):
    place = jnp.stack([lax.axis_index("dom"), lax.axis_index("sub")]).astype(jnp.int32)
    first = jnp.pad(jnp.concatenate([place, row_counts]), (0, neighbours.shape[1] - 3))
    return jnp.concatenate([first[None, :], neighbours, send_count, jnp.swapaxes(send_idx[0], 0, 1)])


def write_outgoing(facts, basis, flip, first, second):
    for slot in range(facts.slots):
        block, sent = facts.send(0, slot)
        flip[slot] = basis[block] * sent.astype(BF16)
        block, sent = facts.send(1, slot)
        far = basis[block] * sent.astype(BF16)
        for pairing, out in enumerate((first, second)):
            block, sent = facts.send(2 + pairing, slot)
            out[slot] = basis[block] * sent.astype(BF16)
            out[facts.slots + slot] = far * facts.relays(pairing, True).astype(BF16)


def outgoing_shapes(slots, dirs, width):
    return [jax.ShapeDtypeStruct((n * slots, dirs, width), BF16) for n in (1, 2, 2)]


def prepare(shape, facts, directions, basis, ways, *outgoing):
    facts = Facts(facts, *shape)
    for pairing in range(2):
        ways[pairing] = jnp.full(ways.shape[1:], facts.relays(pairing, False), F32).astype(BF16)
    for b in range(basis.shape[0]):
        basis[b] = directions[b] * facts.live(b).astype(BF16)
    write_outgoing(facts, basis, *outgoing)


def call_prepare(shape, facts, directions):
    return pl.pallas_call(
        functools.partial(prepare, shape),
        in_specs=[SMEM, VMEM],
        out_specs=[VMEM] * 5,
        out_shape=[
            jax.ShapeDtypeStruct(directions.shape, BF16),
            jax.ShapeDtypeStruct((2, 16, directions.shape[2]), BF16),
        ]
        + outgoing_shapes(shape[1], *directions.shape[1:]),
        compiler_params=SMALL,
        cost_estimate=pl.CostEstimate(flops=8 << 30, bytes_accessed=64 << 20, transcendentals=0),
        name="prepare",
    )(facts, directions)


def pass_on(slots, ways, flip, first, second, out):
    for s in range(slots):
        out[s] = flip[s]
        out[slots + s] = first[slots + s] * ways[0, :1] + second[slots + s] * ways[1, :1]


def call_pass_on(slots, ways, flip, first, second):
    return pl.pallas_call(
        functools.partial(pass_on, slots),
        in_specs=[VMEM] * 4,
        out_specs=VMEM,
        out_shape=jax.ShapeDtypeStruct(first.shape, BF16),
        compiler_params=SMALL,
        name="pass_on",
    )(ways, flip, first, second)


def stack(counts, *refs):
    out, place = refs[-1], 0
    for ref, count in zip(refs, counts):
        for i in range(count):
            out[place + i] = ref[i]
        place += count


def call_stack(pieces, counts, after=()):
    return pl.pallas_call(
        functools.partial(stack, counts),
        in_specs=[VMEM] * len(pieces) + [ANY] * len(after),
        out_specs=VMEM,
        out_shape=jax.ShapeDtypeStruct((sum(counts),) + pieces[0].shape[1:], pieces[0].dtype),
        compiler_params=SMALL,
        name="stack",
    )(*pieces, *after)


def forward_adjoint(shape, relatives, sources, facts, cols, tiles, friction, *refs):
    neigh, slots = shape
    count = len(relatives)
    inputs = 1 + max(ref for places in sources for ref, _ in places)
    parts, refs = refs[:inputs], refs[inputs:]
    keep, send, grams = refs[:3]
    facts = Facts(facts, neigh, slots)
    blocks, tiles_row, width = tiles.shape[0], tiles.shape[1], tiles.shape[2]
    dirs = grams.shape[0]
    live_rows = facts.live_rows()
    columns, total, weights, pieces = refs[3:]

    own_base = [jnp.bitwise_xor(facts.sub(), r) * blocks for r in relatives]
    halo_base = [
        [
            count * blocks + (jnp.bitwise_xor(facts.sub(), r) * neigh + facts.colour(i)) * slots
            for i in range(neigh)
        ]
        for r in relatives
    ]
    for (own, first, second), base, bases in zip(sources, own_base, halo_base):
        for i in range(blocks):
            columns[base + i] = parts[own[0]][own[1] + i]
        for i in range(neigh):
            part, place = (first, second)[i // 2]
            for s in range(slots):
                columns[bases[i] + s] = parts[part][place + i % 2 * slots + s]
    total[...] = jnp.zeros_like(total)
    weights[...] = jnp.zeros_like(weights)
    pieces[...] = jnp.zeros_like(pieces)

    def forward(row):
        picked = jnp.concatenate([columns[cols[row, j]] for j in range(tiles_row)], axis=1)
        wide = jnp.concatenate([tiles[row, j] for j in range(tiles_row)], axis=1)
        cut = STREAMED * width
        state = lax.dot_general(wide[:, :cut], picked[:, :cut], NT, preferred_element_type=F32).T
        state += lax.dot_general(picked[:, cut:], wide[:, cut:], NT, preferred_element_type=F32)
        weights[row] = (friction[pl.ds(row, 1), :] * state).astype(BF16)
        pieces[row] = jnp.concatenate(split_bf16(state, 2), axis=1)

    def adjoint(row):
        weighted = weights[row]
        for j in range(0, tiles_row, 2):
            pair = list(range(j, min(j + 2, tiles_row)))
            wide = jnp.concatenate([tiles[row, i] for i in pair], axis=1)
            product = jnp.dot(weighted, wide, preferred_element_type=F32)
            for k, i in enumerate(pair):
                total[cols[row, i]] += product[:, k * width : (k + 1) * width]

    def step(row, carry):
        adjoint(row)
        forward(row + 1)
        return carry

    forward(0)
    lax.fori_loop(0, live_rows - 1, step, 0)
    adjoint(live_rows - 1)

    mine = jnp.concatenate([parts[0][i] for i in range(blocks)], axis=1)
    basis_gram = lax.dot_general(mine, mine, NT, preferred_element_type=F32)
    cross_gram = lax.dot_general(
        jnp.concatenate([pieces[i] for i in range(blocks)], axis=1),
        jnp.concatenate([weights[i // 2] for i in range(2 * blocks)], axis=1),
        NT,
        preferred_element_type=F32,
    )
    grams[:, :dirs] = basis_gram
    grams[:, dirs:] = basis_gram + cross_gram

    half = count // 2
    for out, chosen in ((keep, range(half)), (send, range(half, count))):
        place = 0
        for k in chosen:
            for i in range(blocks):
                out[place + i] = total[own_base[k] + i]
            place += blocks
        for k in chosen:
            for i in range(neigh):
                for s in range(slots):
                    out[place + i * slots + s] = total[halo_base[k][i] + s]
            place += neigh * slots


def call_forward_adjoint(shape, relatives, sources, facts, cols, tiles, friction, parts):
    blocks, tiles_row, width = tiles.shape[0], tiles.shape[1], tiles.shape[2]
    dirs = parts[0].shape[1]
    count = len(relatives)
    own, halo = count * blocks, count * shape[0] * shape[1]
    out = lambda n: jax.ShapeDtypeStruct((n, dirs, width), F32)
    out_shape = [out((own + halo) // 2)] * 2 + [jax.ShapeDtypeStruct((dirs, 2 * dirs), F32)]
    scratch_shapes = [
        pltpu.VMEM((own + halo, dirs, width), BF16),
        pltpu.VMEM((own + halo, dirs, width), F32),
        pltpu.VMEM((blocks, dirs, width), BF16),
        pltpu.VMEM((blocks, dirs, 2 * width), BF16),
    ]
    return pl.pallas_call(
        functools.partial(forward_adjoint, shape, relatives, sources),
        in_specs=[SMEM, SMEM, VMEM, VMEM] + [VMEM] * len(parts),
        out_specs=[VMEM] * len(out_shape),
        out_shape=out_shape,
        scratch_shapes=scratch_shapes,
        compiler_params=pltpu.CompilerParams(vmem_limit_bytes=24 << 20),
        cost_estimate=pl.CostEstimate(
            flops=4 * blocks * tiles_row * width * width * dirs,
            bytes_accessed=blocks * tiles_row * width * width * 2,
            transcendentals=0,
        ),
        name="forward_adjoint",
    )(facts, cols, tiles, friction, *parts)


def join(start, keep, got, *refs):
    near, far = refs[-2:]
    count = near.shape[0]
    for i in range(count):
        near[i] = keep[start + i] + got[start + i]
        far[i] = (keep[start + count + i] + got[start + count + i]).astype(BF16)


def call_join(start, count, keep, got, after):
    shape = (count,) + keep.shape[1:]
    return pl.pallas_call(
        functools.partial(join, start),
        in_specs=[VMEM] * 2 + [ANY] * len(after),
        out_specs=[VMEM] * 2,
        out_shape=[jax.ShapeDtypeStruct(shape, F32), jax.ShapeDtypeStruct(shape, BF16)],
        compiler_params=SMALL,
        name="join",
    )(keep, got, *after)


def hand_back(slots, blocks, keep, got, here, there, near_flip, far_flip, far_pairs, near_pairs):
    pair = 2 * slots
    near = [keep[2 * blocks + i] + got[2 * blocks + i] for i in range(2 * pair)]
    far = [keep[2 * blocks + 2 * pair + i] + got[2 * blocks + 2 * pair + i] for i in range(2 * pair)]
    for i in range(pair):
        near_flip[i] = near[i].astype(BF16)
        far_flip[i] = far[i].astype(BF16)
        far_pairs[i] = far[pair + i].astype(BF16)
        near_pairs[i] = near[pair + i]
    for i, piece in enumerate(split_bf16(here[...] + there[...], 2)):
        for out in (near_flip, far_flip, far_pairs):
            out[pair + i] = piece


def call_hand_back(slots, blocks, keep, got, here, there):
    pair, tail = 2 * slots, keep.shape[1:]
    out = jax.ShapeDtypeStruct((pair + 2,) + tail, BF16)
    return pl.pallas_call(
        functools.partial(hand_back, slots, blocks),
        in_specs=[VMEM] * 4,
        out_specs=[VMEM] * 4,
        out_shape=[out, out, out, jax.ShapeDtypeStruct((pair,) + tail, F32)],
        compiler_params=SMALL,
        name="hand_back",
    )(keep, got, here, there)


def pass_back(slots, ways, sent, flip, flip_far, far, near_pairs, first, second, own):
    pair = 2 * slots
    for s in range(slots):
        own[s] = flip[s].astype(F32) + flip_far[s].astype(F32)
        relayed = (flip[slots + s].astype(F32) + flip_far[slots + s].astype(F32)).astype(BF16)
        for pairing, out in enumerate((first, second)):
            i = pairing * slots + s
            out[s] = (near_pairs[i] + far[i].astype(F32)).astype(BF16)
            out[slots + s] = relayed * ways[pairing, :1]
    grams = (joined(sent, pair) + joined(far, pair)) + (joined(flip, pair) + joined(flip_far, pair))
    for i, piece in enumerate(split_bf16(grams, 2)):
        first[pair + i] = piece


def call_pass_back(slots, ways, sent, flip, flip_far, far, near_pairs):
    pair, tail = 2 * slots, flip.shape[1:]
    out = lambda n, t: jax.ShapeDtypeStruct((n,) + tail, t)
    return pl.pallas_call(
        functools.partial(pass_back, slots),
        in_specs=[VMEM] * 6,
        out_specs=[VMEM] * 3,
        out_shape=[out(pair + 2, BF16), out(pair, BF16), out(slots, F32)],
        compiler_params=SMALL,
        name="pass_back",
    )(ways, sent, flip, flip_far, far, near_pairs)


def eliminate(grams, dirs):
    wide = grams.shape[1]
    panels = [grams[8 * i : 8 * i + 8, :] for i in range(dirs // 8)]
    rows = lax.broadcasted_iota(jnp.int32, (8, wide), 0)

    def spread(x, column):
        return jnp.broadcast_to(x[:, column : column + 1], (8, wide))

    for k in range(dirs // 8):
        pivot = panels[k]
        lead = [spread(pivot, 8 * k + j) for j in range(8)]
        for t in range(8):
            inverse = 1.0 / lead[t][t : t + 1, :]
            row = pivot[t : t + 1, :] * inverse
            pivot = jnp.where(rows == t, row, pivot - lead[t] * row)
            for j in range(t + 1, 8):
                other = lead[j][t : t + 1, :] * inverse
                lead[j] = jnp.where(rows == t, other, lead[j] - lead[t] * other)
        for i in range(dirs // 8):
            if i != k:
                old = panels[i]
                new = old
                for j in range(8):
                    new = new - spread(old, 8 * k + j) * pivot[j : j + 1, :]
                panels[i] = new
        panels[k] = pivot
    return jnp.concatenate(panels, axis=0)[:, dirs:]


def project(shape, last, facts, passed, basis, near_own, far_own, *refs):
    slots = shape[1]
    facts = Facts(facts, *shape)
    flip, pairs, outs, image = refs[0], refs[1:3], refs[3:-1], refs[-1]
    blocks, dirs = basis.shape[0], basis.shape[1]
    for b in range(blocks):
        image[b] = near_own[b] + far_own[b].astype(F32)
    for s in range(slots):
        relayed = sum(x[slots + s].astype(F32) * facts.relays(i, True) for i, x in enumerate(pairs))
        for role, back in enumerate((flip[s], relayed, pairs[0][s], pairs[1][s])):
            block, sent = facts.send(role, s)
            image[block] += back.astype(F32) * sent
    grams = joined(passed, 2 * slots) + joined(pairs[0], 2 * slots)
    coupling = eliminate(grams, dirs)
    turned = jnp.concatenate(split_bf16(coupling.T, 3), axis=1)
    if last:
        outs[1][...] = grams[:, dirs:]
    for b in range(blocks):
        block = basis[b]
        wanted = facts.live(b) * (image[b] + 1.0 * block.astype(F32))
        tall = jnp.concatenate([block] * 3, axis=0)
        rest = wanted - jnp.dot(turned, tall, preferred_element_type=F32)
        outs[0][b] = rest.astype(outs[0].dtype)
    if not last:
        write_outgoing(facts, outs[0], *outs[1:])


def call_project(shape, last, facts, sent, basis, near_own, far_own, returned):
    blocks, dirs, width = basis.shape
    if last:
        out_shape = [jax.ShapeDtypeStruct(basis.shape, F32), jax.ShapeDtypeStruct((dirs, dirs), F32)]
    else:
        out_shape = [jax.ShapeDtypeStruct(basis.shape, BF16)]
        out_shape += outgoing_shapes(shape[1], dirs, width)
    return pl.pallas_call(
        functools.partial(project, shape, last),
        in_specs=[SMEM] + [VMEM] * 7,
        out_specs=[VMEM] * len(out_shape),
        out_shape=out_shape,
        scratch_shapes=[pltpu.VMEM((blocks, dirs, width), F32)],
        cost_estimate=pl.CostEstimate(
            flops=6 * blocks * dirs * dirs * width, bytes_accessed=20 * blocks * dirs * width, transcendentals=0
        ),
        compiler_params=SMALL,
        name="project",
    )(facts, sent, basis, near_own, far_own, *returned)


def on_device(directions, tiles, tile_cols, friction, neighbours, send_idx, send_count, row_counts):
    near, far = bits_of(lax.axis_size("sub"))
    dom_bits = bits_of(lax.axis_size("dom"))
    blocks = directions.shape[0]
    neigh, slots = send_idx.shape[1:]
    shape = (neigh, slots)
    relatives = (0, far, near, near | far)
    facts = pack_facts(neighbours, send_idx, send_count, row_counts)
    basis, ways, *outgoing = call_prepare(shape, facts, directions)
    for step in range(ITERS):
        own_far, own_near = swap(basis, "sub", far), swap(basis, "sub", near)
        pairs = [pair_up(x, i) for i, x in enumerate(outgoing[1:])]
        pair = 2 * slots
        onward = call_pass_on(slots, ways, outgoing[0], *pairs)
        flip, far01 = swap(onward, "dom", dom_bits[0]), swap_both(onward, dom_bits[0], far)
        halo23 = call_stack(pairs, (slots, slots), [own_near, own_far])
        far23 = swap(halo23, "sub", far)
        rest = swap(call_stack([flip, halo23, far01, far23], (pair,) * 4), "sub", near)
        parts = [basis, own_near, own_far, swap(own_far, "sub", near)]
        parts += [flip, halo23, far01, far23, rest]
        sources = (
            ((0, 0), (4, 0), (5, 0)),
            ((2, 0), (6, 0), (7, 0)),
            ((1, 0), (8, 0), (8, pair)),
            ((3, 0), (8, 2 * pair), (8, 3 * pair)),
        )
        keep, send, grams = call_forward_adjoint(
            shape, relatives, sources, facts, tile_cols, tiles, friction, parts
        )
        for bit in dom_bits[2:]:
            grams = grams + swap(grams, "dom", bit)
        got, grams_got = swap(send, "sub", near), swap(grams, "sub", near)
        near_flip, far_flip, far_pairs, near_pairs = call_hand_back(slots, blocks, keep, got, grams, grams_got)
        flip, flip_far = swap(near_flip, "dom", dom_bits[0]), swap_both(far_flip, dom_bits[0], far)
        pairs_got = swap(far_pairs, "sub", far)
        near_own, far_own = call_join(0, blocks, keep, got, [pairs_got])
        far_own_got = swap(far_own, "sub", far)
        *back, flip = call_pass_back(slots, ways, near_flip, flip, flip_far, pairs_got, near_pairs)
        returned = [flip] + [pair_up(x, i) for i, x in enumerate(back)]
        last = step == ITERS - 1
        basis, *outgoing = call_project(
            shape, last, facts, back[0], basis, near_own, far_own_got, returned
        )
    remainder, cross = basis, outgoing[0]
    return (remainder, cross)


def solution(mesh):
    in_specs = (
        P(("dom", "sub"), None, None),
        P(("dom", "sub"), None, None, None),
        P(("dom", "sub"), None),
        P(("dom", "sub"), None),
        P("dom", None),
        P(("dom", "sub"), None, None),
        P(("dom", "sub"), None),
        P(("dom", "sub")),
    )
    out_specs = (P(("dom", "sub"), None, None), P())
    return jax.shard_map(
        on_device, mesh=mesh, in_specs=in_specs, out_specs=out_specs, check_vma=False
    )
```

```python
import functools

import jax
import jax.numpy as jnp
from jax import lax
from jax.experimental import pallas as pl
from jax.experimental.pallas import tpu as pltpu
from jax.sharding import PartitionSpec as P

ITERS = 2
STREAMED = 8
F32 = jnp.float32
BF16 = jnp.bfloat16
NT = (((1,), (1,)), ((), ()))
VMEM = pl.BlockSpec(memory_space=pltpu.VMEM)
SMEM = pl.BlockSpec(memory_space=pltpu.SMEM)
ANY = pl.BlockSpec(memory_space=pl.ANY)
SMALL = pltpu.CompilerParams(vmem_limit_bytes=8 << 20)

PAIRINGS = (lambda p: p % 4 < 2, lambda p: p % 4 >= 2)


def bits_of(count):
    return [1 << b for b in range(count.bit_length() - 1)]


def swap(x, axis, bit):
    peers = lax.axis_size(axis)
    return lax.ppermute(x, axis, [(i, i ^ bit) for i in range(peers)])


def swap_both(x, dom_bit, sub_bit):
    subs = lax.axis_size("sub")
    peers = [(p, s) for p in range(lax.axis_size("dom")) for s in range(subs)]
    pairs = [(p * subs + s, (p ^ dom_bit) * subs + (s ^ sub_bit)) for p, s in peers]
    return lax.ppermute(x, ("dom", "sub"), pairs)


def pair_up(x, pairing):
    low = [p for p in range(lax.axis_size("dom") - 2) if PAIRINGS[pairing](p)]
    return lax.ppermute(x, "dom", [(p, p + 2) for p in low] + [(p + 2, p) for p in low])


def split_bf16(x, pieces):
    out = []
    for _ in range(pieces):
        out.append(x.astype(BF16))
        x = x - out[-1].astype(F32)
    return out


def joined(ref, start):
    return ref[start + 1].astype(F32) + ref[start].astype(F32)


class Facts:
    def __init__(self, ref, neigh, slots):
        self.ref, self.neigh, self.slots = ref, neigh, slots

    def odd(self):
        return self.ref[0, 0] % 2

    def upper(self):
        return (self.ref[0, 0] // 2) % 2

    def sub(self):
        return self.ref[0, 1]

    def live_rows(self):
        return self.ref[0, 2]

    def live(self, block):
        return (block < self.live_rows()).astype(F32)

    def colour(self, role):
        return (self.odd(), 1 - self.odd(), 2 + self.upper(), 3 - self.upper())[role]

    def relays(self, pairing, out):
        down = self.upper() if pairing == 0 else 1 - self.upper()
        return (down != self.odd() if out else down == self.odd()).astype(F32)

    def send(self, role, slot):
        colour = self.colour(role)
        sent = (self.ref[1, colour] >= 0) & (slot < self.ref[2, colour])
        return self.ref[3 + slot, colour], sent.astype(F32)


def pack_facts(neighbours, send_idx, send_count, row_counts):
    place = jnp.stack([lax.axis_index("dom"), lax.axis_index("sub")]).astype(jnp.int32)
    first = jnp.pad(jnp.concatenate([place, row_counts]), (0, neighbours.shape[1] - 3))
    return jnp.concatenate([first[None, :], neighbours, send_count, jnp.swapaxes(send_idx[0], 0, 1)])


def write_outgoing(facts, basis, flip, first, second):
    for slot in range(facts.slots):
        block, sent = facts.send(0, slot)
        flip[slot] = basis[block] * sent.astype(BF16)
        block, sent = facts.send(1, slot)
        far = basis[block] * sent.astype(BF16)
        for pairing, out in enumerate((first, second)):
            block, sent = facts.send(2 + pairing, slot)
            out[slot] = basis[block] * sent.astype(BF16)
            out[facts.slots + slot] = far * facts.relays(pairing, True).astype(BF16)


def outgoing_shapes(slots, dirs, width):
    return [jax.ShapeDtypeStruct((n * slots, dirs, width), BF16) for n in (1, 2, 2)]


def prepare(shape, facts, directions, basis, ways, *outgoing):
    facts = Facts(facts, *shape)
    for pairing in range(2):
        ways[pairing] = jnp.full(ways.shape[1:], facts.relays(pairing, False), F32).astype(BF16)
    for b in range(basis.shape[0]):
        basis[b] = directions[b] * facts.live(b).astype(BF16)
    write_outgoing(facts, basis, *outgoing)


def call_prepare(shape, facts, directions):
    return pl.pallas_call(
        functools.partial(prepare, shape),
        in_specs=[SMEM, VMEM],
        out_specs=[VMEM] * 5,
        out_shape=[
            jax.ShapeDtypeStruct(directions.shape, BF16),
            jax.ShapeDtypeStruct((2, 16, directions.shape[2]), BF16),
        ]
        + outgoing_shapes(shape[1], *directions.shape[1:]),
        compiler_params=SMALL,
        cost_estimate=pl.CostEstimate(flops=8 << 30, bytes_accessed=64 << 20, transcendentals=0),
        name="prepare",
    )(facts, directions)


def pass_on(slots, ways, flip, first, second, out):
    for s in range(slots):
        out[s] = flip[s]
        out[slots + s] = first[slots + s] * ways[0, :1] + second[slots + s] * ways[1, :1]


def call_pass_on(slots, ways, flip, first, second):
    return pl.pallas_call(
        functools.partial(pass_on, slots),
        in_specs=[VMEM] * 4,
        out_specs=VMEM,
        out_shape=jax.ShapeDtypeStruct(first.shape, BF16),
        compiler_params=SMALL,
        name="pass_on",
    )(ways, flip, first, second)


def stack(counts, *refs):
    out, place = refs[-1], 0
    for ref, count in zip(refs, counts):
        for i in range(count):
            out[place + i] = ref[i]
        place += count


def call_stack(pieces, counts, after=()):
    return pl.pallas_call(
        functools.partial(stack, counts),
        in_specs=[VMEM] * len(pieces) + [ANY] * len(after),
        out_specs=VMEM,
        out_shape=jax.ShapeDtypeStruct((sum(counts),) + pieces[0].shape[1:], pieces[0].dtype),
        compiler_params=SMALL,
        name="stack",
    )(*pieces, *after)


def forward_adjoint(shape, relatives, sources, facts, cols, tiles, friction, *refs):
    neigh, slots = shape
    count = len(relatives)
    inputs = 1 + max(ref for places in sources for ref, _ in places)
    parts, refs = refs[:inputs], refs[inputs:]
    keep, send, grams = refs[:3]
    facts = Facts(facts, neigh, slots)
    blocks, tiles_row, width = tiles.shape[0], tiles.shape[1], tiles.shape[2]
    dirs = grams.shape[0]
    live_rows = facts.live_rows()
    columns, total, weights, pieces = refs[3:]

    own_base = [jnp.bitwise_xor(facts.sub(), r) * blocks for r in relatives]
    halo_base = [
        [
            count * blocks + (jnp.bitwise_xor(facts.sub(), r) * neigh + facts.colour(i)) * slots
            for i in range(neigh)
        ]
        for r in relatives
    ]
    for (own, first, second), base, bases in zip(sources, own_base, halo_base):
        for i in range(blocks):
            columns[base + i] = parts[own[0]][own[1] + i]
        for i in range(neigh):
            part, place = (first, second)[i // 2]
            for s in range(slots):
                columns[bases[i] + s] = parts[part][place + i % 2 * slots + s]
    total[...] = jnp.zeros_like(total)
    weights[...] = jnp.zeros_like(weights)
    pieces[...] = jnp.zeros_like(pieces)

    def forward(row):
        picked = jnp.concatenate([columns[cols[row, j]] for j in range(tiles_row)], axis=1)
        wide = jnp.concatenate([tiles[row, j] for j in range(tiles_row)], axis=1)
        cut = STREAMED * width
        state = lax.dot_general(wide[:, :cut], picked[:, :cut], NT, preferred_element_type=F32).T
        state += lax.dot_general(picked[:, cut:], wide[:, cut:], NT, preferred_element_type=F32)
        weights[row] = (friction[pl.ds(row, 1), :] * state).astype(BF16)
        pieces[row] = jnp.concatenate(split_bf16(state, 2), axis=1)

    def adjoint(row):
        weighted = weights[row]
        for j in range(0, tiles_row, 2):
            pair = list(range(j, min(j + 2, tiles_row)))
            wide = jnp.concatenate([tiles[row, i] for i in pair], axis=1)
            product = jnp.dot(weighted, wide, preferred_element_type=F32)
            for k, i in enumerate(pair):
                total[cols[row, i]] += product[:, k * width : (k + 1) * width]

    def step(row, carry):
        adjoint(row)
        forward(row + 1)
        return carry

    forward(0)
    lax.fori_loop(0, live_rows - 1, step, 0)
    adjoint(live_rows - 1)

    mine = jnp.concatenate([parts[0][i] for i in range(blocks)], axis=1)
    basis_gram = lax.dot_general(mine, mine, NT, preferred_element_type=F32)
    cross_gram = lax.dot_general(
        jnp.concatenate([pieces[i] for i in range(blocks)], axis=1),
        jnp.concatenate([weights[i // 2] for i in range(2 * blocks)], axis=1),
        NT,
        preferred_element_type=F32,
    )
    grams[:, :dirs] = basis_gram
    grams[:, dirs:] = basis_gram + cross_gram

    half = count // 2
    for out, chosen in ((keep, range(half)), (send, range(half, count))):
        place = 0
        for k in chosen:
            for i in range(blocks):
                out[place + i] = total[own_base[k] + i]
            place += blocks
        for k in chosen:
            for i in range(neigh):
                for s in range(slots):
                    out[place + i * slots + s] = total[halo_base[k][i] + s]
            place += neigh * slots


def call_forward_adjoint(shape, relatives, sources, facts, cols, tiles, friction, parts):
    blocks, tiles_row, width = tiles.shape[0], tiles.shape[1], tiles.shape[2]
    dirs = parts[0].shape[1]
    count = len(relatives)
    own, halo = count * blocks, count * shape[0] * shape[1]
    out = lambda n: jax.ShapeDtypeStruct((n, dirs, width), F32)
    out_shape = [out((own + halo) // 2)] * 2 + [jax.ShapeDtypeStruct((dirs, 2 * dirs), F32)]
    scratch_shapes = [
        pltpu.VMEM((own + halo, dirs, width), BF16),
        pltpu.VMEM((own + halo, dirs, width), F32),
        pltpu.VMEM((blocks, dirs, width), BF16),
        pltpu.VMEM((blocks, dirs, 2 * width), BF16),
    ]
    return pl.pallas_call(
        functools.partial(forward_adjoint, shape, relatives, sources),
        in_specs=[SMEM, SMEM, VMEM, VMEM] + [VMEM] * len(parts),
        out_specs=[VMEM] * len(out_shape),
        out_shape=out_shape,
        scratch_shapes=scratch_shapes,
        compiler_params=pltpu.CompilerParams(vmem_limit_bytes=24 << 20),
        cost_estimate=pl.CostEstimate(
            flops=4 * blocks * tiles_row * width * width * dirs,
            bytes_accessed=blocks * tiles_row * width * width * 2,
            transcendentals=0,
        ),
        name="forward_adjoint",
    )(facts, cols, tiles, friction, *parts)


def join(start, keep, got, *refs):
    near, far = refs[-2:]
    count = near.shape[0]
    for i in range(count):
        near[i] = keep[start + i] + got[start + i]
        far[i] = (keep[start + count + i] + got[start + count + i]).astype(BF16)


def call_join(start, count, keep, got, after):
    shape = (count,) + keep.shape[1:]
    return pl.pallas_call(
        functools.partial(join, start),
        in_specs=[VMEM] * 2 + [ANY] * len(after),
        out_specs=[VMEM] * 2,
        out_shape=[jax.ShapeDtypeStruct(shape, F32), jax.ShapeDtypeStruct(shape, BF16)],
        compiler_params=SMALL,
        name="join",
    )(keep, got, *after)


def hand_back(slots, blocks, keep, got, here, there, near_flip, far_flip, far_pairs, near_pairs):
    pair = 2 * slots
    near = [keep[2 * blocks + i] + got[2 * blocks + i] for i in range(2 * pair)]
    far = [keep[2 * blocks + 2 * pair + i] + got[2 * blocks + 2 * pair + i] for i in range(2 * pair)]
    for i in range(pair):
        near_flip[i] = near[i].astype(BF16)
        far_flip[i] = far[i].astype(BF16)
        far_pairs[i] = far[pair + i].astype(BF16)
        near_pairs[i] = near[pair + i]
    for i, piece in enumerate(split_bf16(here[...] + there[...], 2)):
        for out in (near_flip, far_flip, far_pairs):
            out[pair + i] = piece


def call_hand_back(slots, blocks, keep, got, here, there):
    pair, tail = 2 * slots, keep.shape[1:]
    out = jax.ShapeDtypeStruct((pair + 2,) + tail, BF16)
    return pl.pallas_call(
        functools.partial(hand_back, slots, blocks),
        in_specs=[VMEM] * 4,
        out_specs=[VMEM] * 4,
        out_shape=[out, out, out, jax.ShapeDtypeStruct((pair,) + tail, F32)],
        compiler_params=SMALL,
        name="hand_back",
    )(keep, got, here, there)


def pass_back(slots, ways, sent, flip, flip_far, far, near_pairs, first, second, own):
    pair = 2 * slots
    for s in range(slots):
        own[s] = flip[s].astype(F32) + flip_far[s].astype(F32)
        relayed = (flip[slots + s].astype(F32) + flip_far[slots + s].astype(F32)).astype(BF16)
        for pairing, out in enumerate((first, second)):
            i = pairing * slots + s
            out[s] = (near_pairs[i] + far[i].astype(F32)).astype(BF16)
            out[slots + s] = relayed * ways[pairing, :1]
    grams = (joined(sent, pair) + joined(far, pair)) + (joined(flip, pair) + joined(flip_far, pair))
    for i, piece in enumerate(split_bf16(grams, 2)):
        first[pair + i] = piece


def call_pass_back(slots, ways, sent, flip, flip_far, far, near_pairs):
    pair, tail = 2 * slots, flip.shape[1:]
    out = lambda n, t: jax.ShapeDtypeStruct((n,) + tail, t)
    return pl.pallas_call(
        functools.partial(pass_back, slots),
        in_specs=[VMEM] * 6,
        out_specs=[VMEM] * 3,
        out_shape=[out(pair + 2, BF16), out(pair, BF16), out(slots, F32)],
        compiler_params=SMALL,
        name="pass_back",
    )(ways, sent, flip, flip_far, far, near_pairs)


def eliminate(grams, dirs):
    wide = grams.shape[1]
    panels = [grams[8 * i : 8 * i + 8, :] for i in range(dirs // 8)]
    rows = lax.broadcasted_iota(jnp.int32, (8, wide), 0)

    def spread(x, column):
        return jnp.broadcast_to(x[:, column : column + 1], (8, wide))

    for k in range(dirs // 8):
        pivot = panels[k]
        lead = [spread(pivot, 8 * k + j) for j in range(8)]
        for t in range(8):
            inverse = 1.0 / lead[t][t : t + 1, :]
            row = pivot[t : t + 1, :] * inverse
            pivot = jnp.where(rows == t, row, pivot - lead[t] * row)
            for j in range(t + 1, 8):
                other = lead[j][t : t + 1, :] * inverse
                lead[j] = jnp.where(rows == t, other, lead[j] - lead[t] * other)
        for i in range(dirs // 8):
            if i != k:
                old = panels[i]
                new = old
                for j in range(8):
                    new = new - spread(old, 8 * k + j) * pivot[j : j + 1, :]
                panels[i] = new
        panels[k] = pivot
    return jnp.concatenate(panels, axis=0)[:, dirs:]


def project(shape, last, facts, passed, basis, near_own, far_own, *refs):
    slots = shape[1]
    facts = Facts(facts, *shape)
    flip, pairs, outs, image = refs[0], refs[1:3], refs[3:-1], refs[-1]
    blocks, dirs = basis.shape[0], basis.shape[1]
    for b in range(blocks):
        image[b] = near_own[b] + far_own[b].astype(F32)
    for s in range(slots):
        relayed = sum(x[slots + s].astype(F32) * facts.relays(i, True) for i, x in enumerate(pairs))
        for role, back in enumerate((flip[s], relayed, pairs[0][s], pairs[1][s])):
            block, sent = facts.send(role, s)
            image[block] += back.astype(F32) * sent
    grams = joined(passed, 2 * slots) + joined(pairs[0], 2 * slots)
    coupling = eliminate(grams, dirs)
    turned = jnp.concatenate(split_bf16(coupling.T, 3), axis=1)
    if last:
        outs[1][...] = grams[:, dirs:]
    for b in range(blocks):
        block = basis[b]
        wanted = facts.live(b) * (image[b] + 1.0 * block.astype(F32))
        tall = jnp.concatenate([block] * 3, axis=0)
        rest = wanted - jnp.dot(turned, tall, preferred_element_type=F32)
        outs[0][b] = rest.astype(outs[0].dtype)
    if not last:
        write_outgoing(facts, outs[0], *outs[1:])


def call_project(shape, last, facts, sent, basis, near_own, far_own, returned):
    blocks, dirs, width = basis.shape
    if last:
        out_shape = [jax.ShapeDtypeStruct(basis.shape, F32), jax.ShapeDtypeStruct((dirs, dirs), F32)]
    else:
        out_shape = [jax.ShapeDtypeStruct(basis.shape, BF16)]
        out_shape += outgoing_shapes(shape[1], dirs, width)
    return pl.pallas_call(
        functools.partial(project, shape, last),
        in_specs=[SMEM] + [VMEM] * 7,
        out_specs=[VMEM] * len(out_shape),
        out_shape=out_shape,
        scratch_shapes=[pltpu.VMEM((blocks, dirs, width), F32)],
        cost_estimate=pl.CostEstimate(
            flops=6 * blocks * dirs * dirs * width, bytes_accessed=20 * blocks * dirs * width, transcendentals=0
        ),
        compiler_params=SMALL,
        name="project",
    )(facts, sent, basis, near_own, far_own, *returned)


def on_device(directions, tiles, tile_cols, friction, neighbours, send_idx, send_count, row_counts):
    near, far = bits_of(lax.axis_size("sub"))
    dom_bits = bits_of(lax.axis_size("dom"))
    blocks = directions.shape[0]
    neigh, slots = send_idx.shape[1:]
    shape = (neigh, slots)
    relatives = (0, far, near, near | far)
    facts = pack_facts(neighbours, send_idx, send_count, row_counts)
    basis, ways, *outgoing = call_prepare(shape, facts, directions)
    for step in range(ITERS):
        own_near = swap(basis, "sub", near)
        pairs = [pair_up(x, i) for i, x in enumerate(outgoing[1:])]
        pair = 2 * slots
        own_far = swap(call_stack([basis], (blocks,), [pairs[0]]), "sub", far)
        onward = call_pass_on(slots, ways, outgoing[0], *pairs)
        flip, far01 = swap(onward, "dom", dom_bits[0]), swap_both(onward, dom_bits[0], far)
        halo23 = call_stack(pairs, (slots, slots), [own_near])
        far23 = swap(halo23, "sub", far)
        rest = swap(call_stack([flip, halo23, far01, far23], (pair,) * 4), "sub", near)
        parts = [basis, own_near, own_far, swap(own_far, "sub", near)]
        parts += [flip, halo23, far01, far23, rest]
        sources = (
            ((0, 0), (4, 0), (5, 0)),
            ((2, 0), (6, 0), (7, 0)),
            ((1, 0), (8, 0), (8, pair)),
            ((3, 0), (8, 2 * pair), (8, 3 * pair)),
        )
        keep, send, grams = call_forward_adjoint(
            shape, relatives, sources, facts, tile_cols, tiles, friction, parts
        )
        for bit in dom_bits[2:]:
            grams = grams + swap(grams, "dom", bit)
        got, grams_got = swap(send, "sub", near), swap(grams, "sub", near)
        near_flip, far_flip, far_pairs, near_pairs = call_hand_back(slots, blocks, keep, got, grams, grams_got)
        flip, flip_far = swap(near_flip, "dom", dom_bits[0]), swap_both(far_flip, dom_bits[0], far)
        pairs_got = swap(far_pairs, "sub", far)
        near_own, far_own = call_join(0, blocks, keep, got, [pairs_got])
        far_own_got = swap(far_own, "sub", far)
        *back, flip = call_pass_back(slots, ways, near_flip, flip, flip_far, pairs_got, near_pairs)
        returned = [flip] + [pair_up(x, i) for i, x in enumerate(back)]
        last = step == ITERS - 1
        basis, *outgoing = call_project(
            shape, last, facts, back[0], basis, near_own, far_own_got, returned
        )
    remainder, cross = basis, outgoing[0]
    return (remainder, cross)


def solution(mesh):
    in_specs = (
        P(("dom", "sub"), None, None),
        P(("dom", "sub"), None, None, None),
        P(("dom", "sub"), None),
        P(("dom", "sub"), None),
        P("dom", None),
        P(("dom", "sub"), None, None),
        P(("dom", "sub"), None),
        P(("dom", "sub")),
    )
    out_specs = (P(("dom", "sub"), None, None), P())
    return jax.shard_map(
        on_device, mesh=mesh, in_specs=in_specs, out_specs=out_specs, check_vma=False
    )
```

```python
import functools

import jax
import jax.numpy as jnp
from jax import lax
from jax.experimental import pallas as pl
from jax.experimental.pallas import tpu as pltpu
from jax.sharding import PartitionSpec as P

ITERS = 2
STREAMED = 8
F32 = jnp.float32
BF16 = jnp.bfloat16
NT = (((1,), (1,)), ((), ()))
VMEM = pl.BlockSpec(memory_space=pltpu.VMEM)
SMEM = pl.BlockSpec(memory_space=pltpu.SMEM)
ANY = pl.BlockSpec(memory_space=pl.ANY)
SMALL = pltpu.CompilerParams(vmem_limit_bytes=8 << 20)

PAIRINGS = (lambda p: p % 4 < 2, lambda p: p % 4 >= 2)


def bits_of(count):
    return [1 << b for b in range(count.bit_length() - 1)]


def swap(x, axis, bit):
    peers = lax.axis_size(axis)
    return lax.ppermute(x, axis, [(i, i ^ bit) for i in range(peers)])


def swap_both(x, dom_bit, sub_bit):
    subs = lax.axis_size("sub")
    peers = [(p, s) for p in range(lax.axis_size("dom")) for s in range(subs)]
    pairs = [(p * subs + s, (p ^ dom_bit) * subs + (s ^ sub_bit)) for p, s in peers]
    return lax.ppermute(x, ("dom", "sub"), pairs)


def pair_up(x, pairing):
    low = [p for p in range(lax.axis_size("dom") - 2) if PAIRINGS[pairing](p)]
    return lax.ppermute(x, "dom", [(p, p + 2) for p in low] + [(p + 2, p) for p in low])


def split_bf16(x, pieces):
    out = []
    for _ in range(pieces):
        out.append(x.astype(BF16))
        x = x - out[-1].astype(F32)
    return out


def joined(ref, start):
    return ref[start + 1].astype(F32) + ref[start].astype(F32)


class Facts:
    def __init__(self, ref, neigh, slots):
        self.ref, self.neigh, self.slots = ref, neigh, slots

    def odd(self):
        return self.ref[0, 0] % 2

    def upper(self):
        return (self.ref[0, 0] // 2) % 2

    def sub(self):
        return self.ref[0, 1]

    def live_rows(self):
        return self.ref[0, 2]

    def live(self, block):
        return (block < self.live_rows()).astype(F32)

    def colour(self, role):
        return (self.odd(), 1 - self.odd(), 2 + self.upper(), 3 - self.upper())[role]

    def relays(self, pairing, out):
        down = self.upper() if pairing == 0 else 1 - self.upper()
        return (down != self.odd() if out else down == self.odd()).astype(F32)

    def send(self, role, slot):
        colour = self.colour(role)
        sent = (self.ref[1, colour] >= 0) & (slot < self.ref[2, colour])
        return self.ref[3 + slot, colour], sent.astype(F32)


def pack_facts(neighbours, send_idx, send_count, row_counts):
    place = jnp.stack([lax.axis_index("dom"), lax.axis_index("sub")]).astype(jnp.int32)
    first = jnp.pad(jnp.concatenate([place, row_counts]), (0, neighbours.shape[1] - 3))
    return jnp.concatenate([first[None, :], neighbours, send_count, jnp.swapaxes(send_idx[0], 0, 1)])


def write_outgoing(facts, basis, flip, first, second):
    for slot in range(facts.slots):
        block, sent = facts.send(0, slot)
        flip[slot] = basis[block] * sent.astype(BF16)
        block, sent = facts.send(1, slot)
        far = basis[block] * sent.astype(BF16)
        for pairing, out in enumerate((first, second)):
            block, sent = facts.send(2 + pairing, slot)
            out[slot] = basis[block] * sent.astype(BF16)
            out[facts.slots + slot] = far * facts.relays(pairing, True).astype(BF16)


def outgoing_shapes(slots, dirs, width):
    return [jax.ShapeDtypeStruct((n * slots, dirs, width), BF16) for n in (1, 2, 2)]


def prepare(shape, facts, directions, basis, ways, *outgoing):
    facts = Facts(facts, *shape)
    for pairing in range(2):
        ways[pairing] = jnp.full(ways.shape[1:], facts.relays(pairing, False), F32).astype(BF16)
    for b in range(basis.shape[0]):
        basis[b] = directions[b] * facts.live(b).astype(BF16)
    write_outgoing(facts, basis, *outgoing)


def call_prepare(shape, facts, directions):
    return pl.pallas_call(
        functools.partial(prepare, shape),
        in_specs=[SMEM, VMEM],
        out_specs=[VMEM] * 5,
        out_shape=[
            jax.ShapeDtypeStruct(directions.shape, BF16),
            jax.ShapeDtypeStruct((2, 16, directions.shape[2]), BF16),
        ]
        + outgoing_shapes(shape[1], *directions.shape[1:]),
        compiler_params=SMALL,
        cost_estimate=pl.CostEstimate(flops=8 << 30, bytes_accessed=64 << 20, transcendentals=0),
        name="prepare",
    )(facts, directions)


def pass_on(slots, ways, flip, first, second, out):
    for s in range(slots):
        out[s] = flip[s]
        out[slots + s] = first[slots + s] * ways[0, :1] + second[slots + s] * ways[1, :1]


def call_pass_on(slots, ways, flip, first, second):
    return pl.pallas_call(
        functools.partial(pass_on, slots),
        in_specs=[VMEM] * 4,
        out_specs=VMEM,
        out_shape=jax.ShapeDtypeStruct(first.shape, BF16),
        compiler_params=SMALL,
        name="pass_on",
    )(ways, flip, first, second)


def stack(counts, *refs):
    out, place = refs[-1], 0
    for ref, count in zip(refs, counts):
        for i in range(count):
            out[place + i] = ref[i]
        place += count


def call_stack(pieces, counts, after=()):
    return pl.pallas_call(
        functools.partial(stack, counts),
        in_specs=[VMEM] * len(pieces) + [ANY] * len(after),
        out_specs=VMEM,
        out_shape=jax.ShapeDtypeStruct((sum(counts),) + pieces[0].shape[1:], pieces[0].dtype),
        compiler_params=SMALL,
        name="stack",
    )(*pieces, *after)


def forward_adjoint(shape, relatives, sources, facts, cols, tiles, friction, *refs):
    neigh, slots = shape
    count = len(relatives)
    inputs = 1 + max(ref for places in sources for ref, _ in places)
    parts, refs = refs[:inputs], refs[inputs:]
    keep, send, grams = refs[:3]
    facts = Facts(facts, neigh, slots)
    blocks, tiles_row, width = tiles.shape[0], tiles.shape[1], tiles.shape[2]
    dirs = grams.shape[0]
    live_rows = facts.live_rows()
    columns, total, weights, pieces = refs[3:]

    own_base = [jnp.bitwise_xor(facts.sub(), r) * blocks for r in relatives]
    halo_base = [
        [
            count * blocks + (jnp.bitwise_xor(facts.sub(), r) * neigh + facts.colour(i)) * slots
            for i in range(neigh)
        ]
        for r in relatives
    ]
    for (own, first, second), base, bases in zip(sources, own_base, halo_base):
        for i in range(blocks):
            columns[base + i] = parts[own[0]][own[1] + i]
        for i in range(neigh):
            part, place = (first, second)[i // 2]
            for s in range(slots):
                columns[bases[i] + s] = parts[part][place + i % 2 * slots + s]
    total[...] = jnp.zeros_like(total)
    weights[...] = jnp.zeros_like(weights)
    pieces[...] = jnp.zeros_like(pieces)

    def forward(row):
        picked = jnp.concatenate([columns[cols[row, j]] for j in range(tiles_row)], axis=1)
        wide = jnp.concatenate([tiles[row, j] for j in range(tiles_row)], axis=1)
        cut = STREAMED * width
        state = lax.dot_general(wide[:, :cut], picked[:, :cut], NT, preferred_element_type=F32).T
        state += lax.dot_general(picked[:, cut:], wide[:, cut:], NT, preferred_element_type=F32)
        weights[row] = (friction[pl.ds(row, 1), :] * state).astype(BF16)
        pieces[row] = jnp.concatenate(split_bf16(state, 2), axis=1)

    def adjoint(row):
        weighted = weights[row]
        for j in range(0, tiles_row, 2):
            pair = list(range(j, min(j + 2, tiles_row)))
            wide = jnp.concatenate([tiles[row, i] for i in pair], axis=1)
            product = jnp.dot(weighted, wide, preferred_element_type=F32)
            for k, i in enumerate(pair):
                total[cols[row, i]] += product[:, k * width : (k + 1) * width]

    def step(row, carry):
        adjoint(row)
        forward(row + 1)
        return carry

    forward(0)
    lax.fori_loop(0, live_rows - 1, step, 0)
    adjoint(live_rows - 1)

    mine = jnp.concatenate([parts[0][i] for i in range(blocks)], axis=1)
    basis_gram = lax.dot_general(mine, mine, NT, preferred_element_type=F32)
    cross_gram = lax.dot_general(
        jnp.concatenate([pieces[i] for i in range(blocks)], axis=1),
        jnp.concatenate([weights[i // 2] for i in range(2 * blocks)], axis=1),
        NT,
        preferred_element_type=F32,
    )
    grams[:, :dirs] = basis_gram
    grams[:, dirs:] = basis_gram + cross_gram

    half = count // 2
    for out, chosen in ((keep, range(half)), (send, range(half, count))):
        place = 0
        for k in chosen:
            for i in range(blocks):
                out[place + i] = total[own_base[k] + i]
            place += blocks
        for k in chosen:
            for i in range(neigh):
                for s in range(slots):
                    out[place + i * slots + s] = total[halo_base[k][i] + s]
            place += neigh * slots


def call_forward_adjoint(shape, relatives, sources, facts, cols, tiles, friction, parts):
    blocks, tiles_row, width = tiles.shape[0], tiles.shape[1], tiles.shape[2]
    dirs = parts[0].shape[1]
    count = len(relatives)
    own, halo = count * blocks, count * shape[0] * shape[1]
    out = lambda n: jax.ShapeDtypeStruct((n, dirs, width), F32)
    out_shape = [out((own + halo) // 2)] * 2 + [jax.ShapeDtypeStruct((dirs, 2 * dirs), F32)]
    scratch_shapes = [
        pltpu.VMEM((own + halo, dirs, width), BF16),
        pltpu.VMEM((own + halo, dirs, width), F32),
        pltpu.VMEM((blocks, dirs, width), BF16),
        pltpu.VMEM((blocks, dirs, 2 * width), BF16),
    ]
    return pl.pallas_call(
        functools.partial(forward_adjoint, shape, relatives, sources),
        in_specs=[SMEM, SMEM, VMEM, VMEM] + [VMEM] * len(parts),
        out_specs=[VMEM] * len(out_shape),
        out_shape=out_shape,
        scratch_shapes=scratch_shapes,
        compiler_params=pltpu.CompilerParams(vmem_limit_bytes=24 << 20),
        cost_estimate=pl.CostEstimate(
            flops=4 * blocks * tiles_row * width * width * dirs,
            bytes_accessed=blocks * tiles_row * width * width * 2,
            transcendentals=0,
        ),
        name="forward_adjoint",
    )(facts, cols, tiles, friction, *parts)


def join(start, keep, got, *refs):
    near, far = refs[-2:]
    count = near.shape[0]
    for i in range(count):
        near[i] = keep[start + i] + got[start + i]
        far[i] = (keep[start + count + i] + got[start + count + i]).astype(BF16)


def call_join(start, count, keep, got, after):
    shape = (count,) + keep.shape[1:]
    return pl.pallas_call(
        functools.partial(join, start),
        in_specs=[VMEM] * 2 + [ANY] * len(after),
        out_specs=[VMEM] * 2,
        out_shape=[jax.ShapeDtypeStruct(shape, F32), jax.ShapeDtypeStruct(shape, BF16)],
        compiler_params=SMALL,
        name="join",
    )(keep, got, *after)


def hand_back(slots, blocks, keep, got, here, there, near_flip, far_flip, far_pairs, near_pairs):
    pair = 2 * slots
    near = [keep[2 * blocks + i] + got[2 * blocks + i] for i in range(2 * pair)]
    far = [keep[2 * blocks + 2 * pair + i] + got[2 * blocks + 2 * pair + i] for i in range(2 * pair)]
    for i in range(pair):
        near_flip[i] = near[i].astype(BF16)
        far_flip[i] = far[i].astype(BF16)
        far_pairs[i] = far[pair + i].astype(BF16)
        near_pairs[i] = near[pair + i]
    for i, piece in enumerate(split_bf16(here[...] + there[...], 2)):
        for out in (near_flip, far_flip, far_pairs):
            out[pair + i] = piece


def call_hand_back(slots, blocks, keep, got, here, there):
    pair, tail = 2 * slots, keep.shape[1:]
    out = jax.ShapeDtypeStruct((pair + 2,) + tail, BF16)
    return pl.pallas_call(
        functools.partial(hand_back, slots, blocks),
        in_specs=[VMEM] * 4,
        out_specs=[VMEM] * 4,
        out_shape=[out, out, out, jax.ShapeDtypeStruct((pair,) + tail, F32)],
        compiler_params=SMALL,
        name="hand_back",
    )(keep, got, here, there)


def pass_back(slots, ways, sent, flip, flip_far, far, near_pairs, first, second, own):
    pair = 2 * slots
    for s in range(slots):
        own[s] = flip[s].astype(F32) + flip_far[s].astype(F32)
        relayed = (flip[slots + s].astype(F32) + flip_far[slots + s].astype(F32)).astype(BF16)
        for pairing, out in enumerate((first, second)):
            i = pairing * slots + s
            out[s] = (near_pairs[i] + far[i].astype(F32)).astype(BF16)
            out[slots + s] = relayed * ways[pairing, :1]
    grams = (joined(sent, pair) + joined(far, pair)) + (joined(flip, pair) + joined(flip_far, pair))
    for i, piece in enumerate(split_bf16(grams, 2)):
        first[pair + i] = piece


def call_pass_back(slots, ways, sent, flip, flip_far, far, near_pairs):
    pair, tail = 2 * slots, flip.shape[1:]
    out = lambda n, t: jax.ShapeDtypeStruct((n,) + tail, t)
    return pl.pallas_call(
        functools.partial(pass_back, slots),
        in_specs=[VMEM] * 6,
        out_specs=[VMEM] * 3,
        out_shape=[out(pair + 2, BF16), out(pair, BF16), out(slots, F32)],
        compiler_params=SMALL,
        name="pass_back",
    )(ways, sent, flip, flip_far, far, near_pairs)


def eliminate(grams, dirs):
    wide = grams.shape[1]
    panels = [grams[8 * i : 8 * i + 8, :] for i in range(dirs // 8)]
    rows = lax.broadcasted_iota(jnp.int32, (8, wide), 0)

    def spread(x, column):
        return jnp.broadcast_to(x[:, column : column + 1], (8, wide))

    for k in range(dirs // 8):
        pivot = panels[k]
        lead = [spread(pivot, 8 * k + j) for j in range(8)]
        for t in range(8):
            inverse = 1.0 / lead[t][t : t + 1, :]
            row = pivot[t : t + 1, :] * inverse
            pivot = jnp.where(rows == t, row, pivot - lead[t] * row)
            for j in range(t + 1, 8):
                other = lead[j][t : t + 1, :] * inverse
                lead[j] = jnp.where(rows == t, other, lead[j] - lead[t] * other)
        for i in range(dirs // 8):
            if i != k:
                old = panels[i]
                new = old
                for j in range(8):
                    new = new - spread(old, 8 * k + j) * pivot[j : j + 1, :]
                panels[i] = new
        panels[k] = pivot
    return jnp.concatenate(panels, axis=0)[:, dirs:]


def solve(start, sent, got, coupling, cross):
    grams = joined(sent, start) + joined(got, start)
    dirs = grams.shape[0]
    coupling[...] = jnp.concatenate(split_bf16(eliminate(grams, dirs).T, 3), axis=1)
    cross[...] = grams[:, dirs:]


def call_solve(start, sent, got):
    dirs = sent.shape[1]
    return pl.pallas_call(
        functools.partial(solve, start),
        in_specs=[VMEM] * 2,
        out_specs=[VMEM] * 2,
        out_shape=[jax.ShapeDtypeStruct((dirs, 3 * dirs), BF16), jax.ShapeDtypeStruct((dirs, dirs), F32)],
        compiler_params=SMALL,
        cost_estimate=pl.CostEstimate(flops=4 * dirs**3, bytes_accessed=16 * dirs * dirs, transcendentals=dirs),
        name="solve",
    )(sent, got)


def project(shape, last, facts, coupling, basis, near_own, far_own, *refs):
    slots = shape[1]
    facts = Facts(facts, *shape)
    flip, pairs, outs, image = refs[0], refs[1:3], refs[3:-1], refs[-1]
    blocks = basis.shape[0]
    for b in range(blocks):
        image[b] = near_own[b] + far_own[b].astype(F32)
    for s in range(slots):
        relayed = sum(x[slots + s].astype(F32) * facts.relays(i, True) for i, x in enumerate(pairs))
        for role, back in enumerate((flip[s], relayed, pairs[0][s], pairs[1][s])):
            block, sent = facts.send(role, s)
            image[block] += back.astype(F32) * sent
    for b in range(blocks):
        block = basis[b]
        wanted = facts.live(b) * (image[b] + 1.0 * block.astype(F32))
        tall = jnp.concatenate([block] * 3, axis=0)
        rest = wanted - jnp.dot(coupling[...], tall, preferred_element_type=F32)
        outs[0][b] = rest.astype(outs[0].dtype)
    if not last:
        write_outgoing(facts, outs[0], *outs[1:])


def call_project(shape, last, facts, coupling, basis, near_own, far_own, returned):
    blocks, dirs, width = basis.shape
    if last:
        out_shape = [jax.ShapeDtypeStruct(basis.shape, F32)]
    else:
        out_shape = [jax.ShapeDtypeStruct(basis.shape, BF16)]
        out_shape += outgoing_shapes(shape[1], dirs, width)
    return pl.pallas_call(
        functools.partial(project, shape, last),
        in_specs=[SMEM] + [VMEM] * 7,
        out_specs=[VMEM] * len(out_shape),
        out_shape=out_shape,
        scratch_shapes=[pltpu.VMEM((blocks, dirs, width), F32)],
        cost_estimate=pl.CostEstimate(
            flops=6 * blocks * dirs * dirs * width, bytes_accessed=20 * blocks * dirs * width, transcendentals=0
        ),
        compiler_params=SMALL,
        name="project",
    )(facts, coupling, basis, near_own, far_own, *returned)


def on_device(directions, tiles, tile_cols, friction, neighbours, send_idx, send_count, row_counts):
    near, far = bits_of(lax.axis_size("sub"))
    dom_bits = bits_of(lax.axis_size("dom"))
    blocks = directions.shape[0]
    neigh, slots = send_idx.shape[1:]
    shape = (neigh, slots)
    relatives = (0, far, near, near | far)
    facts = pack_facts(neighbours, send_idx, send_count, row_counts)
    basis, ways, *outgoing = call_prepare(shape, facts, directions)
    for step in range(ITERS):
        own_near = swap(basis, "sub", near)
        pairs = [pair_up(x, i) for i, x in enumerate(outgoing[1:])]
        pair = 2 * slots
        own_far = swap(call_stack([basis], (blocks,), [pairs[0]]), "sub", far)
        onward = call_pass_on(slots, ways, outgoing[0], *pairs)
        flip, far01 = swap(onward, "dom", dom_bits[0]), swap_both(onward, dom_bits[0], far)
        halo23 = call_stack(pairs, (slots, slots), [own_near])
        far23 = swap(halo23, "sub", far)
        rest = swap(call_stack([flip, halo23, far01, far23], (pair,) * 4), "sub", near)
        parts = [basis, own_near, own_far, swap(own_far, "sub", near)]
        parts += [flip, halo23, far01, far23, rest]
        sources = (
            ((0, 0), (4, 0), (5, 0)),
            ((2, 0), (6, 0), (7, 0)),
            ((1, 0), (8, 0), (8, pair)),
            ((3, 0), (8, 2 * pair), (8, 3 * pair)),
        )
        keep, send, grams = call_forward_adjoint(
            shape, relatives, sources, facts, tile_cols, tiles, friction, parts
        )
        for bit in dom_bits[2:]:
            grams = grams + swap(grams, "dom", bit)
        got, grams_got = swap(send, "sub", near), swap(grams, "sub", near)
        near_flip, far_flip, far_pairs, near_pairs = call_hand_back(slots, blocks, keep, got, grams, grams_got)
        flip, flip_far = swap(near_flip, "dom", dom_bits[0]), swap_both(far_flip, dom_bits[0], far)
        pairs_got = swap(far_pairs, "sub", far)
        near_own, far_own = call_join(0, blocks, keep, got, [pairs_got])
        far_own_got = swap(far_own, "sub", far)
        *back, flip = call_pass_back(slots, ways, near_flip, flip, flip_far, pairs_got, near_pairs)
        returned = [flip] + [pair_up(x, i) for i, x in enumerate(back)]
        coupling, cross = call_solve(2 * slots, back[0], returned[1])
        last = step == ITERS - 1
        basis, *outgoing = call_project(
            shape, last, facts, coupling, basis, near_own, far_own_got, returned
        )
    return (basis, cross)


def solution(mesh):
    in_specs = (
        P(("dom", "sub"), None, None),
        P(("dom", "sub"), None, None, None),
        P(("dom", "sub"), None),
        P(("dom", "sub"), None),
        P("dom", None),
        P(("dom", "sub"), None, None),
        P(("dom", "sub"), None),
        P(("dom", "sub")),
    )
    out_specs = (P(("dom", "sub"), None, None), P())
    return jax.shard_map(
        on_device, mesh=mesh, in_specs=in_specs, out_specs=out_specs, check_vma=False
    )
```

```python
import functools

import jax
import jax.numpy as jnp
from jax import lax
from jax.experimental import pallas as pl
from jax.experimental.pallas import tpu as pltpu
from jax.sharding import PartitionSpec as P

ITERS = 2
STREAMED = 8
F32 = jnp.float32
BF16 = jnp.bfloat16
NT = (((1,), (1,)), ((), ()))
VMEM = pl.BlockSpec(memory_space=pltpu.VMEM)
SMEM = pl.BlockSpec(memory_space=pltpu.SMEM)
ANY = pl.BlockSpec(memory_space=pl.ANY)
SMALL = pltpu.CompilerParams(vmem_limit_bytes=8 << 20)

PAIRINGS = (lambda p: p % 4 < 2, lambda p: p % 4 >= 2)


def bits_of(count):
    return [1 << b for b in range(count.bit_length() - 1)]


def swap(x, axis, bit):
    peers = lax.axis_size(axis)
    return lax.ppermute(x, axis, [(i, i ^ bit) for i in range(peers)])


def swap_both(x, dom_bit, sub_bit):
    subs = lax.axis_size("sub")
    peers = [(p, s) for p in range(lax.axis_size("dom")) for s in range(subs)]
    pairs = [(p * subs + s, (p ^ dom_bit) * subs + (s ^ sub_bit)) for p, s in peers]
    return lax.ppermute(x, ("dom", "sub"), pairs)


def pair_up(x, pairing):
    low = [p for p in range(lax.axis_size("dom") - 2) if PAIRINGS[pairing](p)]
    return lax.ppermute(x, "dom", [(p, p + 2) for p in low] + [(p + 2, p) for p in low])


def split_bf16(x, pieces):
    out = []
    for _ in range(pieces):
        out.append(x.astype(BF16))
        x = x - out[-1].astype(F32)
    return out


def joined(ref, start):
    return ref[start + 1].astype(F32) + ref[start].astype(F32)


class Facts:
    def __init__(self, ref, neigh, slots):
        self.ref, self.neigh, self.slots = ref, neigh, slots

    def odd(self):
        return self.ref[0, 0] % 2

    def upper(self):
        return (self.ref[0, 0] // 2) % 2

    def sub(self):
        return self.ref[0, 1]

    def live_rows(self):
        return self.ref[0, 2]

    def live(self, block):
        return (block < self.live_rows()).astype(F32)

    def colour(self, role):
        return (self.odd(), 1 - self.odd(), 2 + self.upper(), 3 - self.upper())[role]

    def relays(self, pairing, out):
        down = self.upper() if pairing == 0 else 1 - self.upper()
        return (down != self.odd() if out else down == self.odd()).astype(F32)

    def send(self, role, slot):
        colour = self.colour(role)
        sent = (self.ref[1, colour] >= 0) & (slot < self.ref[2, colour])
        return self.ref[3 + slot, colour], sent.astype(F32)


def pack_facts(neighbours, send_idx, send_count, row_counts):
    place = jnp.stack([lax.axis_index("dom"), lax.axis_index("sub")]).astype(jnp.int32)
    first = jnp.pad(jnp.concatenate([place, row_counts]), (0, neighbours.shape[1] - 3))
    return jnp.concatenate([first[None, :], neighbours, send_count, jnp.swapaxes(send_idx[0], 0, 1)])


def write_outgoing(facts, basis, flip, first, second):
    for slot in range(facts.slots):
        block, sent = facts.send(0, slot)
        flip[slot] = basis[block] * sent.astype(BF16)
        block, sent = facts.send(1, slot)
        far = basis[block] * sent.astype(BF16)
        for pairing, out in enumerate((first, second)):
            block, sent = facts.send(2 + pairing, slot)
            out[slot] = basis[block] * sent.astype(BF16)
            out[facts.slots + slot] = far * facts.relays(pairing, True).astype(BF16)


def outgoing_shapes(slots, dirs, width):
    return [jax.ShapeDtypeStruct((n * slots, dirs, width), BF16) for n in (1, 2, 2)]


def prepare(shape, facts, directions, basis, ways, *outgoing):
    facts = Facts(facts, *shape)
    for pairing in range(2):
        ways[pairing] = jnp.full(ways.shape[1:], facts.relays(pairing, False), F32).astype(BF16)
    for b in range(basis.shape[0]):
        basis[b] = directions[b] * facts.live(b).astype(BF16)
    write_outgoing(facts, basis, *outgoing)


def call_prepare(shape, facts, directions):
    return pl.pallas_call(
        functools.partial(prepare, shape),
        in_specs=[SMEM, VMEM],
        out_specs=[VMEM] * 5,
        out_shape=[
            jax.ShapeDtypeStruct(directions.shape, BF16),
            jax.ShapeDtypeStruct((2,) + directions.shape[1:], BF16),
        ]
        + outgoing_shapes(shape[1], *directions.shape[1:]),
        compiler_params=SMALL,
        cost_estimate=pl.CostEstimate(flops=8 << 30, bytes_accessed=64 << 20, transcendentals=0),
        name="prepare",
    )(facts, directions)


def pass_on(slots, ways, flip, first, second, out):
    for s in range(slots):
        out[s] = flip[s]
        out[slots + s] = first[slots + s] * ways[0] + second[slots + s] * ways[1]


def call_pass_on(slots, ways, flip, first, second):
    return pl.pallas_call(
        functools.partial(pass_on, slots),
        in_specs=[VMEM] * 4,
        out_specs=VMEM,
        out_shape=jax.ShapeDtypeStruct(first.shape, BF16),
        compiler_params=SMALL,
        name="pass_on",
    )(ways, flip, first, second)


def stack(counts, *refs):
    out, place = refs[-1], 0
    for ref, count in zip(refs, counts):
        for i in range(count):
            out[place + i] = ref[i]
        place += count


def call_stack(pieces, counts, after=()):
    return pl.pallas_call(
        functools.partial(stack, counts),
        in_specs=[VMEM] * len(pieces) + [ANY] * len(after),
        out_specs=VMEM,
        out_shape=jax.ShapeDtypeStruct((sum(counts),) + pieces[0].shape[1:], pieces[0].dtype),
        compiler_params=SMALL,
        name="stack",
    )(*pieces, *after)


def forward_adjoint(shape, relatives, sources, facts, cols, tiles, friction, *refs):
    neigh, slots = shape
    count = len(relatives)
    inputs = 1 + max(ref for places in sources for ref, _ in places)
    parts, refs = refs[:inputs], refs[inputs:]
    keep, send, grams = refs[:3]
    facts = Facts(facts, neigh, slots)
    blocks, tiles_row, width = tiles.shape[0], tiles.shape[1], tiles.shape[2]
    dirs = grams.shape[0]
    live_rows = facts.live_rows()
    columns, total, weights, pieces = refs[3:]

    own_base = [jnp.bitwise_xor(facts.sub(), r) * blocks for r in relatives]
    halo_base = [
        [
            count * blocks + (jnp.bitwise_xor(facts.sub(), r) * neigh + facts.colour(i)) * slots
            for i in range(neigh)
        ]
        for r in relatives
    ]
    for (own, first, second), base, bases in zip(sources, own_base, halo_base):
        for i in range(blocks):
            columns[base + i] = parts[own[0]][own[1] + i]
        for i in range(neigh):
            part, place = (first, second)[i // 2]
            for s in range(slots):
                columns[bases[i] + s] = parts[part][place + i % 2 * slots + s]
    total[...] = jnp.zeros_like(total)
    weights[...] = jnp.zeros_like(weights)
    pieces[...] = jnp.zeros_like(pieces)

    def forward(row):
        picked = jnp.concatenate([columns[cols[row, j]] for j in range(tiles_row)], axis=1)
        wide = jnp.concatenate([tiles[row, j] for j in range(tiles_row)], axis=1)
        cut = STREAMED * width
        state = lax.dot_general(wide[:, :cut], picked[:, :cut], NT, preferred_element_type=F32).T
        state += lax.dot_general(picked[:, cut:], wide[:, cut:], NT, preferred_element_type=F32)
        weights[row] = (friction[pl.ds(row, 1), :] * state).astype(BF16)
        pieces[row] = jnp.concatenate(split_bf16(state, 2), axis=1)

    def adjoint(row):
        weighted = weights[row]
        for j in range(0, tiles_row, 2):
            pair = list(range(j, min(j + 2, tiles_row)))
            wide = jnp.concatenate([tiles[row, i] for i in pair], axis=1)
            product = jnp.dot(weighted, wide, preferred_element_type=F32)
            for k, i in enumerate(pair):
                total[cols[row, i]] += product[:, k * width : (k + 1) * width]

    def step(row, carry):
        adjoint(row)
        forward(row + 1)
        return carry

    forward(0)
    lax.fori_loop(0, live_rows - 1, step, 0)
    adjoint(live_rows - 1)

    mine = jnp.concatenate([parts[0][i] for i in range(blocks)], axis=1)
    basis_gram = lax.dot_general(mine, mine, NT, preferred_element_type=F32)
    cross_gram = lax.dot_general(
        jnp.concatenate([pieces[i] for i in range(blocks)], axis=1),
        jnp.concatenate([weights[i // 2] for i in range(2 * blocks)], axis=1),
        NT,
        preferred_element_type=F32,
    )
    grams[:, :dirs] = basis_gram
    grams[:, dirs:] = basis_gram + cross_gram

    half = count // 2
    for out, chosen in ((keep, range(half)), (send, range(half, count))):
        place = 0
        for k in chosen:
            for i in range(blocks):
                out[place + i] = total[own_base[k] + i]
            place += blocks
        for k in chosen:
            for i in range(neigh):
                for s in range(slots):
                    out[place + i * slots + s] = total[halo_base[k][i] + s]
            place += neigh * slots


def call_forward_adjoint(shape, relatives, sources, facts, cols, tiles, friction, parts):
    blocks, tiles_row, width = tiles.shape[0], tiles.shape[1], tiles.shape[2]
    dirs = parts[0].shape[1]
    count = len(relatives)
    own, halo = count * blocks, count * shape[0] * shape[1]
    out = lambda n: jax.ShapeDtypeStruct((n, dirs, width), F32)
    out_shape = [out((own + halo) // 2)] * 2 + [jax.ShapeDtypeStruct((dirs, 2 * dirs), F32)]
    scratch_shapes = [
        pltpu.VMEM((own + halo, dirs, width), BF16),
        pltpu.VMEM((own + halo, dirs, width), F32),
        pltpu.VMEM((blocks, dirs, width), BF16),
        pltpu.VMEM((blocks, dirs, 2 * width), BF16),
    ]
    return pl.pallas_call(
        functools.partial(forward_adjoint, shape, relatives, sources),
        in_specs=[SMEM, SMEM, VMEM, VMEM] + [VMEM] * len(parts),
        out_specs=[VMEM] * len(out_shape),
        out_shape=out_shape,
        scratch_shapes=scratch_shapes,
        compiler_params=pltpu.CompilerParams(vmem_limit_bytes=24 << 20),
        cost_estimate=pl.CostEstimate(
            flops=4 * blocks * tiles_row * width * width * dirs,
            bytes_accessed=blocks * tiles_row * width * width * 2,
            transcendentals=0,
        ),
        name="forward_adjoint",
    )(facts, cols, tiles, friction, *parts)


def join(start, keep, got, *refs):
    near, far = refs[-2:]
    count = near.shape[0]
    for i in range(count):
        near[i] = keep[start + i] + got[start + i]
        far[i] = (keep[start + count + i] + got[start + count + i]).astype(BF16)


def call_join(start, count, keep, got, after):
    shape = (count,) + keep.shape[1:]
    return pl.pallas_call(
        functools.partial(join, start),
        in_specs=[VMEM] * 2 + [ANY] * len(after),
        out_specs=[VMEM] * 2,
        out_shape=[jax.ShapeDtypeStruct(shape, F32), jax.ShapeDtypeStruct(shape, BF16)],
        compiler_params=SMALL,
        name="join",
    )(keep, got, *after)


def hand_back(slots, blocks, keep, got, grams, near_flip, far_flip, far_pairs, near_pairs):
    pair = 2 * slots
    near = [keep[2 * blocks + i] + got[2 * blocks + i] for i in range(2 * pair)]
    far = [keep[2 * blocks + 2 * pair + i] + got[2 * blocks + 2 * pair + i] for i in range(2 * pair)]
    for i in range(pair):
        near_flip[i] = near[i].astype(BF16)
        far_flip[i] = far[i].astype(BF16)
        far_pairs[i] = far[pair + i].astype(BF16)
        near_pairs[i] = near[pair + i]
    for i, piece in enumerate(split_bf16(grams[...], 2)):
        for out in (near_flip, far_flip, far_pairs):
            out[pair + i] = piece


def call_hand_back(slots, blocks, keep, got, grams):
    pair, tail = 2 * slots, keep.shape[1:]
    out = jax.ShapeDtypeStruct((pair + 2,) + tail, BF16)
    return pl.pallas_call(
        functools.partial(hand_back, slots, blocks),
        in_specs=[VMEM] * 3,
        out_specs=[VMEM] * 4,
        out_shape=[out, out, out, jax.ShapeDtypeStruct((pair,) + tail, F32)],
        compiler_params=SMALL,
        name="hand_back",
    )(keep, got, grams)


def pass_back(slots, ways, sent, flip, flip_far, far, near_pairs, first, second, own):
    pair = 2 * slots
    for s in range(slots):
        own[s] = flip[s].astype(F32) + flip_far[s].astype(F32)
        relayed = (flip[slots + s].astype(F32) + flip_far[slots + s].astype(F32)).astype(BF16)
        for pairing, out in enumerate((first, second)):
            i = pairing * slots + s
            out[s] = (near_pairs[i] + far[i].astype(F32)).astype(BF16)
            out[slots + s] = relayed * ways[pairing]
    grams = (joined(sent, pair) + joined(far, pair)) + (joined(flip, pair) + joined(flip_far, pair))
    for i, piece in enumerate(split_bf16(grams, 2)):
        first[pair + i] = piece


def call_pass_back(slots, ways, sent, flip, flip_far, far, near_pairs):
    pair, tail = 2 * slots, flip.shape[1:]
    out = lambda n, t: jax.ShapeDtypeStruct((n,) + tail, t)
    return pl.pallas_call(
        functools.partial(pass_back, slots),
        in_specs=[VMEM] * 6,
        out_specs=[VMEM] * 3,
        out_shape=[out(pair + 2, BF16), out(pair, BF16), out(slots, F32)],
        compiler_params=SMALL,
        name="pass_back",
    )(ways, sent, flip, flip_far, far, near_pairs)


def eliminate(grams, dirs):
    wide = grams.shape[1]
    panels = [grams[8 * i : 8 * i + 8, :] for i in range(dirs // 8)]
    rows = lax.broadcasted_iota(jnp.int32, (8, wide), 0)

    def spread(x, column):
        return jnp.broadcast_to(x[:, column : column + 1], (8, wide))

    for k in range(dirs // 8):
        pivot = panels[k]
        lead = [spread(pivot, 8 * k + j) for j in range(8)]
        for t in range(8):
            inverse = 1.0 / lead[t][t : t + 1, :]
            row = pivot[t : t + 1, :] * inverse
            pivot = jnp.where(rows == t, row, pivot - lead[t] * row)
            for j in range(t + 1, 8):
                other = lead[j][t : t + 1, :] * inverse
                lead[j] = jnp.where(rows == t, other, lead[j] - lead[t] * other)
        for i in range(dirs // 8):
            if i != k:
                old = panels[i]
                new = old
                for j in range(8):
                    new = new - spread(old, 8 * k + j) * pivot[j : j + 1, :]
                panels[i] = new
        panels[k] = pivot
    return jnp.concatenate(panels, axis=0)[:, dirs:]


def sum_grams(start, sent, got, out):
    out[...] = joined(sent, start) + joined(got, start)


def call_sum_grams(start, sent, got):
    return pl.pallas_call(
        functools.partial(sum_grams, start),
        in_specs=[VMEM] * 2,
        out_specs=VMEM,
        out_shape=jax.ShapeDtypeStruct(sent.shape[1:], F32),
        compiler_params=SMALL,
        name="sum_grams",
    )(sent, got)


def solve(here, there, coupling, *cross):
    grams = here[...] + there[...]
    dirs = grams.shape[0]
    coupling[...] = jnp.concatenate(split_bf16(eliminate(grams, dirs).T, 3), axis=1)
    for out in cross:
        out[...] = grams[:, dirs:]


def call_solve(last, here, there):
    dirs = here.shape[0]
    out_shape = [jax.ShapeDtypeStruct((dirs, 3 * dirs), BF16)]
    if last:
        out_shape.append(jax.ShapeDtypeStruct((dirs, dirs), F32))
    return pl.pallas_call(
        solve,
        in_specs=[VMEM] * 2,
        out_specs=[VMEM] * len(out_shape),
        out_shape=out_shape,
        compiler_params=SMALL,
        cost_estimate=pl.CostEstimate(flops=4 * dirs**3, bytes_accessed=16 * dirs * dirs, transcendentals=dirs),
        name="solve",
    )(here, there)


def project(shape, last, facts, coupling, basis, near_own, far_own, *refs):
    slots = shape[1]
    facts = Facts(facts, *shape)
    flip, pairs, outs, image = refs[0], refs[1:3], refs[3:-1], refs[-1]
    blocks = basis.shape[0]
    for b in range(blocks):
        image[b] = near_own[b] + far_own[b].astype(F32)
    for s in range(slots):
        relayed = sum(x[slots + s].astype(F32) * facts.relays(i, True) for i, x in enumerate(pairs))
        for role, back in enumerate((flip[s], relayed, pairs[0][s], pairs[1][s])):
            block, sent = facts.send(role, s)
            image[block] += back.astype(F32) * sent
    for b in range(blocks):
        block = basis[b]
        wanted = facts.live(b) * (image[b] + 1.0 * block.astype(F32))
        tall = jnp.concatenate([block] * 3, axis=0)
        rest = wanted - jnp.dot(coupling[...], tall, preferred_element_type=F32)
        outs[0][b] = rest.astype(outs[0].dtype)
    if not last:
        write_outgoing(facts, outs[0], *outs[1:])


def call_project(shape, last, facts, coupling, basis, near_own, far_own, returned):
    blocks, dirs, width = basis.shape
    if last:
        out_shape = [jax.ShapeDtypeStruct(basis.shape, F32)]
    else:
        out_shape = [jax.ShapeDtypeStruct(basis.shape, BF16)]
        out_shape += outgoing_shapes(shape[1], dirs, width)
    return pl.pallas_call(
        functools.partial(project, shape, last),
        in_specs=[SMEM] + [VMEM] * 7,
        out_specs=[VMEM] * len(out_shape),
        out_shape=out_shape,
        scratch_shapes=[pltpu.VMEM((blocks, dirs, width), F32)],
        cost_estimate=pl.CostEstimate(
            flops=6 * blocks * dirs * dirs * width, bytes_accessed=20 * blocks * dirs * width, transcendentals=0
        ),
        compiler_params=SMALL,
        name="project",
    )(facts, coupling, basis, near_own, far_own, *returned)


def on_device(directions, tiles, tile_cols, friction, neighbours, send_idx, send_count, row_counts):
    near, far = bits_of(lax.axis_size("sub"))
    dom_bits = bits_of(lax.axis_size("dom"))
    blocks = directions.shape[0]
    neigh, slots = send_idx.shape[1:]
    shape = (neigh, slots)
    relatives = (0, far, near, near | far)
    facts = pack_facts(neighbours, send_idx, send_count, row_counts)
    basis, ways, *outgoing = call_prepare(shape, facts, directions)
    for step in range(ITERS):
        own_near = swap(basis, "sub", near)
        pairs = [pair_up(x, i) for i, x in enumerate(outgoing[1:])]
        pair = 2 * slots
        own_far = swap(call_stack([basis], (blocks,), [pairs[0]]), "sub", far)
        onward = call_pass_on(slots, ways, outgoing[0], *pairs)
        flip, far01 = swap(onward, "dom", dom_bits[0]), swap_both(onward, dom_bits[0], far)
        halo23 = call_stack(pairs, (slots, slots), [own_near])
        far23 = swap(halo23, "sub", far)
        rest = swap(call_stack([flip, halo23, far01, far23], (pair,) * 4), "sub", near)
        parts = [basis, own_near, own_far, swap(own_far, "sub", near)]
        parts += [flip, halo23, far01, far23, rest]
        sources = (
            ((0, 0), (4, 0), (5, 0)),
            ((2, 0), (6, 0), (7, 0)),
            ((1, 0), (8, 0), (8, pair)),
            ((3, 0), (8, 2 * pair), (8, 3 * pair)),
        )
        keep, send, grams = call_forward_adjoint(
            shape, relatives, sources, facts, tile_cols, tiles, friction, parts
        )
        for bit in dom_bits[2:]:
            grams = grams + swap(grams, "dom", bit)
        got = swap(send, "sub", near)
        near_flip, far_flip, far_pairs, near_pairs = call_hand_back(slots, blocks, keep, got, grams)
        flip, flip_far = swap(near_flip, "dom", dom_bits[0]), swap_both(far_flip, dom_bits[0], far)
        pairs_got = swap(far_pairs, "sub", far)
        near_own, far_own = call_join(0, blocks, keep, got, [pairs_got])
        far_own_got = swap(far_own, "sub", far)
        *back, flip = call_pass_back(slots, ways, near_flip, flip, flip_far, pairs_got, near_pairs)
        returned = [flip] + [pair_up(x, i) for i, x in enumerate(back)]
        grams = call_sum_grams(2 * slots, back[0], returned[1])
        last = step == ITERS - 1
        coupling, *cross = call_solve(last, grams, swap(grams, "sub", near))
        basis, *outgoing = call_project(
            shape, last, facts, coupling, basis, near_own, far_own_got, returned
        )
    return (basis, cross[0])


def solution(mesh):
    in_specs = (
        P(("dom", "sub"), None, None),
        P(("dom", "sub"), None, None, None),
        P(("dom", "sub"), None),
        P(("dom", "sub"), None),
        P("dom", None),
        P(("dom", "sub"), None, None),
        P(("dom", "sub"), None),
        P(("dom", "sub")),
    )
    out_specs = (P(("dom", "sub"), None, None), P())
    return jax.shard_map(
        on_device, mesh=mesh, in_specs=in_specs, out_specs=out_specs, check_vma=False
    )
```
